32 devices in a mesh: groups: 2 (over x), slab: 16 (over z, y, core).
Axes of the slice: x: 2, y: 2, z: 4, core: 2. Of those that a mesh axis runs over, the one named last changes fastest.
Arguments:
- point_feat: bfloat16 [65536, 64], P(('groups', 'slab')), parts along dimension 0, may hold values from -6 to 6
- point_pos: float32 [3, 65536], P(None, ('groups', 'slab')), parts along dimension 1, may hold values from 0 to 128
- pair_point: int32 [32, 16, 256], P(('groups', 'slab')), parts along dimension 0, may hold values from -1 to 2044, as said below
- pair_cell: int32 [32, 16, 256], P(('groups', 'slab')), parts along dimension 0, may hold values from -1 to 131071, as said below
- lift_weight: bfloat16 [64, 64], replicated, may hold values from -0.75 to 0.75
- spectral_weight: bfloat16 [32, 32, 32, 2, 64, 64], P(None, None, 'slab'), may hold values from -28 to 28
- skip_weight: bfloat16 [64, 64], replicated, may hold values from -0.75 to 0.75
- proj_weight: bfloat16 [64, 64], replicated, may hold values from -0.75 to 0.75
Outputs:
- point_out: bfloat16 [65536, 64], P(('groups', 'slab')), parts along dimension 0
The draws below stay inside these ranges and needn't reach their ends.
There are 2 independent parts, one for each index of `groups`. The reference program is written for one: setup_inputs(seed, part) draws one part's arguments, and reference() takes and returns one part's arrays. A program takes and returns all parts, laid end to end along the dimension named above; an argument that names none is the same for every part. Nothing has to cross between parts.
Inputs may be any that keep to these rules, and one draw needn't show every extreme that they name: `pair_point`: index of a point among the 2048 points of region r, or -1 in an empty slot; a slot is empty here exactly where pair_cell is -1, and the live slots of each list come first. The list of each region to its own slab is full; each region has live lists to exactly five slabs, its own among them. `pair_cell`: index (plane * 128 + y) * 128 + z of a cell within slab s, plane counted within the slab, or -1 in an empty slot.
All inputs are finite; a program needn't handle non-finite values.
Results may differ from the reference program's by a relative error of at most 0.012.
Values may be sent and summed in bfloat16 or wider, within the bound.
A program may use at most 320 MiB of HBM per device.

```python
import jax
import jax.numpy as jnp
from jax import lax

G = 128
C = 64
M = 32
P_DEV = 2048
CAP = 256
PX = 8
RADIUS = 2
POINTS = 32768
N_SLAB = 16


def home_shifts():
    return jnp.array([0, 1, N_SLAB - 1, N_SLAB // 2, N_SLAB // 2 - 1], dtype=jnp.int32)


def surface_cells(key):
    first, second, third = jax.random.split(key, 3)
    index = jnp.arange(POINTS)
    region = index // P_DEV
    local = index % P_DEV
    home = (region + home_shifts()[local % 5]) % N_SLAB
    x_cell = home * PX + jax.random.randint(first, (POINTS,), 0, PX)
    y_cell = jax.random.randint(second, (POINTS,), 0, G)
    tent = jnp.abs(2 * y_cell % G - G // 2)
    z_cell = jnp.clip(G // 4 + tent + jax.random.randint(third, (POINTS,), -1, 2), 0, G - 1)
    return (x_cell, y_cell, z_cell)


def pair_lists(key):
    x_cell, y_cell, z_cell = surface_cells(key)
    inner = jax.random.fold_in(key, 101)
    first, second, third, fourth = jax.random.split(inner, 4)
    source = jnp.arange(N_SLAB)[:, None]
    target = jnp.arange(N_SLAB)[None, :]
    offset = (target - source) % N_SLAB
    matches = offset[:, :, None] == home_shifts()[None, None, :]
    nearby = jnp.any(matches, axis=2)
    which = jnp.sum(matches.astype(jnp.int32) * jnp.arange(5)[None, None, :], axis=2)
    counts = jnp.where(nearby, jax.random.randint(first, (N_SLAB, N_SLAB), CAP // 4, CAP + 1), 0)
    counts = jnp.where(offset == 0, CAP, counts)
    slots = jnp.arange(CAP)[None, None, :]
    filled = counts[:, :, None] > slots
    groups_count = P_DEV // 5
    chosen = jax.random.randint(second, (N_SLAB, N_SLAB, CAP), 0, groups_count)
    chosen = jnp.where(slots == 0, groups_count - 1, chosen)
    local = 5 * chosen + which[:, :, None]
    whole = source[:, :, None] * P_DEV + local
    plane = jnp.clip(x_cell[whole] - (target * PX)[:, :, None], 0, PX - 1)
    near_y = jnp.clip(y_cell[whole] + jax.random.randint(third, (N_SLAB, N_SLAB, CAP), -2, 3), 0, G - 1)
    near_z = jnp.clip(z_cell[whole] + jax.random.randint(fourth, (N_SLAB, N_SLAB, CAP), -2, 3), 0, G - 1)
    cell = (plane * G + near_y) * G + near_z
    corner = (slots == 0) & (offset == 0)[:, :, None]
    cell = jnp.where(corner, PX * G * G - 1, cell)
    return (jnp.where(filled, local, -1).astype(jnp.int32), jnp.where(filled, cell, -1).astype(jnp.int32))


def draw_point_pos(key, part):
    x_cell, y_cell, z_cell = surface_cells(key)
    key = jax.random.fold_in(key, 7)
    fraction = jax.random.uniform(key, (3, POINTS), jnp.float32, 0.02, 0.98)
    return jnp.stack([x_cell, y_cell, z_cell]).astype(jnp.float32) + fraction


def draw_pair_point(key, part):
    return pair_lists(key)[0]


def draw_pair_cell(key, part):
    return pair_lists(key)[1]


def levels(key, extent, shards, low, high):
    def one(axis_at, blocks):
        heights = jax.random.uniform(jax.random.fold_in(jax.random.fold_in(key, 6), axis_at), (blocks,), jnp.float32, low / len(shards), high / len(shards))
        return jnp.repeat(jnp.exp(heights), extent[axis_at] // blocks).reshape((-1,) + (1,) * (len(extent) - axis_at - 1))

    gain = one(*shards[0])
    for cut in shards[1:]:
        gain = gain * one(*cut)
    return gain


def normal_values(own_key, shape, scale, bound, cuts=(), kind=jnp.bfloat16):
    values = jax.random.normal(own_key, shape, jnp.float32) * scale
    if len(cuts) > 0:
        values = levels(own_key, shape, cuts, -0.22, 0.18) * values
    return jnp.clip(values, min=-bound, max=bound).astype(kind)


def setup_inputs(seed: int = 0, part: int = 0) -> dict:
    seeds = jax.random.split(jax.random.key(seed), 9)
    own_keys = jax.random.split(jax.random.fold_in(seeds[8], part), 9)
    return {
        "point_feat": normal_values(own_keys[0], (POINTS, C), 1.0, 6.0, ((0, 16),)),
        "point_pos": draw_point_pos(jax.random.fold_in(jax.random.fold_in(seeds[8], part), 71), part),
        "pair_point": draw_pair_point(jax.random.fold_in(jax.random.fold_in(seeds[8], part), 71), part),
        "pair_cell": draw_pair_cell(jax.random.fold_in(jax.random.fold_in(seeds[8], part), 71), part),
        "lift_weight": normal_values(seeds[4], (C, C), C ** -0.5, 0.75),
        "spectral_weight": normal_values(seeds[5], (M, M, M, 2, C, C), (0.6 * (G // M) ** 1.5), 28.0, ((2, 16),)),
        "skip_weight": normal_values(seeds[6], (C, C), C ** -0.5, 0.75),
        "proj_weight": normal_values(seeds[7], (C, C), C ** -0.5, 0.75),
    }


def mode_tables(length, modes):
    offsets = jnp.arange(modes)
    frequency = jnp.where(offsets < modes // 2, offsets, offsets - modes).astype(jnp.float32)
    places = jnp.arange(length).astype(jnp.float32)
    phase = (2.0 * jnp.pi / length) * (frequency[:, None] * places[None, :])
    return jnp.cos(phase), jnp.sin(phase)


def along(table, tensor, dimension, table_axis):
    product = jnp.tensordot(table, tensor, axes=((table_axis,), (dimension,)), precision=lax.Precision.HIGHEST)
    return jnp.moveaxis(product, 0, dimension)


def forward(real_part, imag_part, dimension, tables):
    cosine, sine = tables
    if imag_part is None:
        return along(cosine, real_part, dimension, 1), -along(sine, real_part, dimension, 1)
    new_real = along(cosine, real_part, dimension, 1) + along(sine, imag_part, dimension, 1)
    new_imag = along(cosine, imag_part, dimension, 1) - along(sine, real_part, dimension, 1)
    return new_real, new_imag


def inverse(real_part, imag_part, dimension, tables, length, keep_imag):
    cosine, sine = tables
    new_real = (along(cosine, real_part, dimension, 0) - along(sine, imag_part, dimension, 0)) / length
    if not keep_imag:
        return new_real
    new_imag = (along(cosine, imag_part, dimension, 0) + along(sine, real_part, dimension, 0)) / length
    return new_real, new_imag


def mix_slice(operands):
    real_part, imag_part, weights = operands
    real_b = real_part.astype(jnp.bfloat16)
    imag_b = imag_part.astype(jnp.bfloat16)
    first = jnp.stack([real_b, -imag_b], axis=2).astype(jnp.float32)
    second = jnp.stack([imag_b, real_b], axis=2).astype(jnp.float32)
    weight_float = weights.astype(jnp.float32)
    new_real = jnp.einsum("bcsd,bcsde->bce", first, weight_float, precision=lax.Precision.HIGHEST)
    new_imag = jnp.einsum("bcsd,bcsde->bce", second, weight_float, precision=lax.Precision.HIGHEST)
    return new_real, new_imag


def pair_weights(positions, cell_ids, slab_first, pair_live):
    centre_x = (cell_ids // (G * G) + slab_first).astype(jnp.float32) + 0.5
    centre_y = ((cell_ids // G) % G).astype(jnp.float32) + 0.5
    centre_z = (cell_ids % G).astype(jnp.float32) + 0.5
    distance = (positions[0] - centre_x) ** 2 + (positions[1] - centre_y) ** 2 + (positions[2] - centre_z) ** 2
    kernel = 1.0 / (1.0 + distance / float(RADIUS * RADIUS))
    return jnp.where(pair_live, kernel, 0.0).astype(jnp.bfloat16)


def reference(point_feat, point_pos, pair_point, pair_cell, lift_weight, spectral_weight, skip_weight, proj_weight):
    planes = G // N_SLAB
    pair_live = pair_cell >= 0
    point_ids = jnp.maximum(pair_point, 0) + (jnp.arange(N_SLAB) * P_DEV).astype(jnp.int32)[:, None, None]
    cell_ids = jnp.maximum(pair_cell, 0)
    slab_first = (jnp.arange(N_SLAB) * planes).astype(jnp.int32)[None, :, None]
    positions = point_pos[:, point_ids]
    weights = pair_weights(positions, cell_ids, slab_first, pair_live)
    grid_ids = (cell_ids + slab_first * (G * G)).reshape(-1)
    flat_points = point_ids.reshape(-1)
    weight_float = weights.astype(jnp.float32).reshape(-1)
    features = point_feat[flat_points].astype(jnp.float32)
    cell_sum = jax.ops.segment_sum(weight_float[:, None] * features, grid_ids, num_segments=G * G * G)
    weight_sum = jax.ops.segment_sum(weight_float, grid_ids, num_segments=G * G * G)
    normalized = (cell_sum / (1.0 + weight_sum)[:, None]).astype(jnp.bfloat16)
    lifted = jnp.dot(normalized, lift_weight, preferred_element_type=jnp.float32).astype(jnp.bfloat16)
    skip_part = jnp.dot(lifted, skip_weight, preferred_element_type=jnp.float32)
    grid_tables = mode_tables(G, M)
    real_part, imag_part = forward(lifted.reshape(G, G, G, C).astype(jnp.float32), None, 2, grid_tables)
    real_part, imag_part = forward(real_part, imag_part, 1, grid_tables)
    real_part, imag_part = forward(real_part, imag_part, 0, grid_tables)
    real_part, imag_part = lax.map(mix_slice, (real_part, imag_part, spectral_weight))
    real_part, imag_part = inverse(real_part, imag_part, 0, grid_tables, G, True)
    real_part, imag_part = inverse(real_part, imag_part, 1, grid_tables, G, True)
    spectral_part = inverse(real_part, imag_part, 2, grid_tables, G, False)
    hidden = jax.nn.gelu(spectral_part.reshape(-1, C) + skip_part).astype(jnp.bfloat16)
    returned = hidden[grid_ids].astype(jnp.float32)
    point_sum = jax.ops.segment_sum(weight_float[:, None] * returned, flat_points, num_segments=POINTS)
    point_weight = jax.ops.segment_sum(weight_float, flat_points, num_segments=POINTS)
    point_mean = (point_sum / (1.0 + point_weight)[:, None]).astype(jnp.bfloat16)
    return jnp.dot(point_mean, proj_weight, preferred_element_type=jnp.float32).astype(jnp.bfloat16)
```

```python
import functools

import jax
import jax.numpy as jnp
from jax import lax
from jax.experimental import pallas as pl
from jax.experimental.pallas import tpu as pltpu
from jax.sharding import PartitionSpec as P

G = 128
C = 64
M = 32
RADIUS = 2
LISTS = 5
CAP = 256
VMEM_LIMIT = 48 * 1024 * 1024
F32 = jnp.float32
BF16 = jnp.bfloat16


def params():
    return pltpu.CompilerParams(vmem_limit_bytes=VMEM_LIMIT)


def frequencies(count, first=0):
    k = first + jnp.arange(count)
    return jnp.where(k < M // 2, k, k - M)


def waves(frequency, length):
    phase = (frequency[:, None] * jnp.arange(length)[None, :]) % length
    angle = (2.0 * jnp.pi / length) * phase.astype(F32)
    return jnp.cos(angle), jnp.sin(angle)


def nt_dot(left, right):
    return lax.dot_general(left, right, (((1,), (1,)), ((), ())), preferred_element_type=F32)


def dot(left, right):
    return jnp.dot(left, right, preferred_element_type=F32)


def prep_kernel(feat_ref, pos_ref, point_ref, cell_ref, slab_ref, lift_ref, lifted_ref, meta_ref, planes):
    points = feat_ref.shape[1]
    pos = pos_ref[...]
    high = pos.astype(BF16)
    rest = pos - high.astype(F32)
    middle = rest.astype(BF16)
    low = (rest - middle.astype(F32)).astype(BF16)
    lift = lift_ref[...]
    feat = feat_ref[...]
    for k in range(LISTS):
        place = pl.ds(k * CAP, CAP)
        point = point_ref[k : k + 1, :]
        cell = cell_ref[k : k + 1, :]
        live = cell >= 0
        cell = jnp.maximum(cell, 0)
        rows = lax.broadcasted_iota(jnp.int32, (points, CAP), 0)
        hot = jnp.where(rows == point, 1.0, 0.0).astype(BF16)
        got = dot(feat, hot).astype(BF16)
        lifted_ref[:, place] = lax.dot_general(
            lift, got, (((0,), (0,)), ((), ())), preferred_element_type=F32
        ).astype(BF16)
        at = dot(high, hot) + dot(middle, hot) + dot(low, hot)
        x = cell // (G * G) + slab_ref[k : k + 1, :] * planes
        y = cell // G % G
        z = cell % G
        xf, yf, zf = x.astype(F32), y.astype(F32), z.astype(F32)
        distance = (
            (at[0:1] - (xf + 0.5)) ** 2 + (at[1:2] - (yf + 0.5)) ** 2 + (at[2:3] - (zf + 0.5)) ** 2
        )
        kernel = 1.0 / (1.0 + distance / float(RADIUS * RADIUS))
        weight = jnp.where(live, kernel, 0.0)
        meta_ref[:, place] = jnp.concatenate(
            [xf, yf, zf, weight, jnp.zeros((12, CAP), F32)], axis=0
        ).astype(BF16)


def share_kernel(slab_ref, key_ref, weight_ref, share_ref, bucket, count):
    lists = key_ref.shape[0]
    slabs = count.shape[0]

    def clear(s, _):
        count[s] = 0
        return 0

    lax.fori_loop(0, slabs, clear, 0)

    def fill(i, _):
        s = slab_ref[i]
        n = count[s]
        bucket[s * lists + n] = i
        count[s] = n + 1
        return 0

    lax.fori_loop(0, lists, fill, 0)
    share_ref[...] = jnp.zeros_like(share_ref)

    def per_slab(s, _):
        n = count[s]

        def per_source(q, _):
            j = bucket[s * lists + q]
            both = jnp.concatenate([key_ref[j], weight_ref[j], jnp.zeros((6, CAP), F32)], axis=0)
            turned = both.T
            key = turned[:, 0:1]
            weight = turned[:, 1:2]

            def per_target(p, _):
                i = bucket[s * lists + p]
                terms = jnp.where(key == key_ref[i], weight, 0.0)
                share_ref[i] += jnp.sum(terms, axis=0, keepdims=True)
                return 0

            return lax.fori_loop(0, n, per_target, 0)

        return lax.fori_loop(0, n, per_source, 0)

    lax.fori_loop(0, slabs, per_slab, 0)
    share_ref[...] = weight_ref[...] / (1.0 + share_ref[...])


def forward_kernel(slab_ref, lifted_ref, meta_ref, share_ref, tab_y_ref, tab_z_ref, planes_ref, wave_ref, total, planes):
    region = pl.program_id(0)
    rows = wave_ref.shape[1]

    @pl.when(region == 0)
    def _():
        total[...] = jnp.zeros_like(total)

    for k in range(LISTS):
        place = pl.ds(k * CAP, CAP)
        slab = slab_ref[region * LISTS + k]
        meta = meta_ref[0, :, place].astype(F32)
        line = lax.broadcasted_iota(jnp.int32, (G, CAP), 0).astype(F32)
        hot_y = jnp.where(line == meta[1:2], 1.0, 0.0).astype(BF16)
        hot_z = jnp.where(line == meta[2:3], 1.0, 0.0).astype(BF16)
        along_y = dot(tab_y_ref[...], hot_y)
        along_z = dot(tab_z_ref[...], hot_z)
        wave = along_y[:rows] * along_z[:rows] + along_y[rows:] * along_z[rows:]
        wave = wave.astype(BF16)
        wave_ref[0, :, place] = wave
        scaled = (lifted_ref[0, :, place].astype(F32) * share_ref[k]).astype(BF16)
        local = meta[0:1] - (slab * planes).astype(F32)
        parts = [
            scaled * jnp.where(local == float(p), 1.0, 0.0).astype(BF16) for p in range(planes)
        ]
        total[slab] += nt_dot(jnp.concatenate(parts, axis=0), wave)

    @pl.when(region == pl.num_programs(0) - 1)
    def _():
        planes_ref[...] = total[...].astype(BF16)


def mix_kernel(coefficient_ref, weight_ref, out_ref):
    columns, depth = weight_ref.shape[1], coefficient_ref.shape[-1]
    for b in range(columns):
        weights = weight_ref[0, b].reshape(depth, C)
        out_ref[0, b] = dot(coefficient_ref[0, b], weights)


def inverse_kernel(slab_ref, meta_ref, wave_ref, field_ref, out_ref, planes):
    region = pl.program_id(0)
    for k in range(LISTS):
        place = pl.ds(k * CAP, CAP)
        slab = slab_ref[region * LISTS + k]
        local = meta_ref[0, :, place].astype(F32)[0:1] - (slab * planes).astype(F32)
        values = dot(field_ref[slab], wave_ref[0, :, place])
        total = jnp.zeros((C, CAP), F32)
        for p in range(planes):
            total += jnp.where(local == float(p), values[p * C : (p + 1) * C], 0.0)
        out_ref[0, :, place] = total.astype(BF16)


def cell_kernel(slab_ref, own_slab_ref, lifted_ref, share_ref, key_ref, own_key_ref, out_ref):
    regions = lifted_ref.shape[0]
    for k in range(LISTS):
        place = pl.ds(k * CAP, CAP)
        out_ref[:, place] = jnp.zeros((C, CAP), F32)
        own = own_key_ref[k : k + 1, :]
        turned = jnp.broadcast_to(own, (8, CAP)).T[:, 0:1]
        slab = own_slab_ref[k]

        def per_region(r, _):
            for m in range(LISTS):

                @pl.when(slab_ref[r * LISTS + m] == slab)
                def _():
                    same = jnp.where(turned == key_ref[r * LISTS + m], 1.0, 0.0).astype(BF16)
                    terms = lifted_ref[r, :, pl.ds(m * CAP, CAP)].astype(F32) * share_ref[r * LISTS + m]
                    out_ref[:, place] += nt_dot(terms.astype(BF16), same)

            return 0

        lax.fori_loop(0, regions, per_region, 0)


def decode_kernel(spectral_ref, cell_ref, meta_ref, point_ref, skip_ref, proj_ref, out_ref):
    points = out_ref.shape[1]
    total = jnp.zeros((C + 16, points), F32)
    for k in range(LISTS):
        place = pl.ds(k * CAP, CAP)
        skip = lax.dot_general(
            skip_ref[...],
            cell_ref[:, place].astype(BF16),
            (((0,), (0,)), ((), ())),
            preferred_element_type=F32,
        )
        u = spectral_ref[:, place].astype(F32) + skip
        hidden = 0.5 * u * (1.0 + jnp.tanh(0.7978845608028654 * (u + 0.044715 * u * u * u)))
        hidden = jnp.concatenate([hidden, jnp.ones((16, CAP), F32)], axis=0).astype(BF16)
        weight = meta_ref[:, place].astype(F32)[3:4]
        rows = lax.broadcasted_iota(jnp.int32, (points, CAP), 0)
        hot = jnp.where(rows == point_ref[k : k + 1, :], weight, 0.0).astype(BF16)
        total += nt_dot(hidden, hot)
    mean = (total[:C] / (1.0 + total[C : C + 1])).astype(BF16)
    out_ref[...] = lax.dot_general(
        proj_ref[...], mean, (((0,), (0,)), ((), ())), preferred_element_type=F32
    ).astype(BF16)


def compact(lists, live):
    rank = jnp.cumsum(live.astype(jnp.int32)) - 1
    hot = live[None, :] & (rank[None, :] == jnp.arange(LISTS)[:, None])
    return jnp.sum(jnp.where(hot[:, :, None], lists[None] + 1, 0), axis=1) - 1, hot


def pad8(array):
    return jnp.concatenate([array, jnp.full((8 - LISTS, array.shape[1]), -1, array.dtype)], axis=0)


VMEM = pl.BlockSpec(memory_space=pltpu.VMEM)
SMEM = pl.BlockSpec(memory_space=pltpu.SMEM)


def shards(
    point_feat,
    point_pos,
    pair_point,
    pair_cell,
    lift_weight,
    spectral_weight,
    skip_weight,
    proj_weight,
):
    slabs = lax.axis_size("slab")
    me = lax.axis_index("slab")
    planes = G // slabs
    own_modes = spectral_weight.shape[2]
    rows = 2 * M * own_modes
    slots = LISTS * CAP
    lists = slabs * LISTS
    points = point_feat.shape[0]

    live = pair_cell[0, :, 0] >= 0
    cells, hot = compact(pair_cell[0], live)
    point_ids, _ = compact(pair_point[0], live)
    own_slab = jnp.sum(jnp.where(hot, jnp.arange(slabs)[None, :], 0), axis=1).astype(jnp.int32)
    cells, point_ids = pad8(cells), pad8(point_ids)
    slab_rows = jnp.broadcast_to(own_slab[:, None], (LISTS, CAP))

    lifted, meta = pl.pallas_call(
        functools.partial(prep_kernel, planes=planes),
        out_shape=(
            jax.ShapeDtypeStruct((C, slots), BF16),
            jax.ShapeDtypeStruct((16, slots), BF16),
        ),
        in_specs=[VMEM] * 6,
        out_specs=(VMEM, VMEM),
        compiler_params=params(),
        name="prep",
    )(point_feat.T, point_pos, point_ids, cells, pad8(slab_rows), lift_weight)

    all_meta = lax.all_gather(meta, "slab")
    all_lifted = lax.all_gather(lifted, "slab")

    def keys(values):
        values = values.astype(F32)
        return (values[..., 0, :] * G + values[..., 1, :]) * G + values[..., 2, :]

    key = keys(all_meta).reshape(lists, 1, CAP)
    weight = all_meta[:, 3].astype(F32).reshape(lists, 1, CAP)
    slab_ids = (all_meta[:, 0, ::CAP].astype(jnp.int32) // planes).reshape(lists)
    own_key = pad8(keys(meta).reshape(LISTS, CAP))

    share = pl.pallas_call(
        share_kernel,
        out_shape=jax.ShapeDtypeStruct((lists, 1, CAP), F32),
        in_specs=[SMEM, VMEM, VMEM],
        out_specs=VMEM,
        scratch_shapes=[
            pltpu.SMEM((slabs * lists,), jnp.int32),
            pltpu.SMEM((slabs,), jnp.int32),
        ],
        compiler_params=params(),
        name="share",
    )(slab_ids, key, weight)

    cos_y, sin_y = waves(frequencies(M), G)
    cos_z, sin_z = waves(frequencies(own_modes, me * own_modes), G)
    cos_b, sin_b = jnp.repeat(cos_y, own_modes, 0), jnp.repeat(sin_y, own_modes, 0)
    cos_c, sin_c = jnp.tile(cos_z, (2 * M, 1)), jnp.tile(sin_z, (2 * M, 1))
    tab_y = jnp.concatenate([cos_b, -sin_b, -sin_b, -cos_b], 0).astype(BF16)
    tab_z = jnp.concatenate([cos_c, sin_c], 0).astype(BF16)

    def region_block(height):
        return pl.BlockSpec((1, height, slots), lambda r, ids: (r, 0, 0))

    def whole(shape):
        return pl.BlockSpec(shape, lambda r, ids: (0,) * len(shape))

    plane_sums, wave = pl.pallas_call(
        functools.partial(forward_kernel, planes=planes),
        out_shape=(
            jax.ShapeDtypeStruct((slabs, planes * C, rows), BF16),
            jax.ShapeDtypeStruct((slabs, rows, slots), BF16),
        ),
        grid_spec=pltpu.PrefetchScalarGridSpec(
            num_scalar_prefetch=1,
            grid=(slabs,),
            in_specs=[
                region_block(C),
                region_block(16),
                pl.BlockSpec((LISTS, 1, CAP), lambda r, ids: (r, 0, 0)),
                whole((2 * rows, G)),
                whole((2 * rows, G)),
            ],
            out_specs=(whole((slabs, planes * C, rows)), region_block(rows)),
            scratch_shapes=[pltpu.VMEM((slabs, planes * C, rows), F32)],
        ),
        compiler_params=params(),
        name="forward",
    )(slab_ids, all_lifted, all_meta, share, tab_y, tab_z)

    real_row = jnp.stack([cos_y, sin_y], 1)
    imag_row = jnp.stack([-sin_y, cos_y], 1)
    analysis = jnp.stack(
        [jnp.stack([real_row, -imag_row]), jnp.stack([imag_row, real_row])]
    ).astype(BF16)
    plane_sums = plane_sums.reshape(G, C, 2, M, own_modes)
    coefficients = jnp.einsum(
        "wsarx,xdrbc->abcwsd", analysis, plane_sums, preferred_element_type=F32
    ).astype(BF16)
    same = jnp.eye(own_modes, dtype=BF16)
    coefficients = coefficients[:, :, :, :, None] * same[:, None, :, None, None]
    coefficients = coefficients.reshape(M, M, 2 * own_modes, own_modes * 2 * C)
    coefficients = jnp.pad(coefficients, ((0, 0), (0, 0), (0, 8 - 2 * own_modes), (0, 0)))

    filtered = pl.pallas_call(
        mix_kernel,
        out_shape=jax.ShapeDtypeStruct((M, M, 8, C), F32),
        grid=(M,),
        in_specs=[
            pl.BlockSpec((1, M, 8, own_modes * 2 * C), lambda a: (a, 0, 0, 0)),
            pl.BlockSpec((1, M, own_modes, 2, C, C), lambda a: (a, 0, 0, 0, 0, 0)),
        ],
        out_specs=pl.BlockSpec((1, M, 8, C), lambda a: (a, 0, 0, 0)),
        compiler_params=params(),
        name="mix",
    )(coefficients, spectral_weight)

    filtered = filtered[:, :, : 2 * own_modes].reshape(M, M, own_modes, 2, C).astype(BF16)
    synthesis = jnp.stack([jnp.stack([cos_y, -sin_y]), jnp.stack([sin_y, cos_y])])
    synthesis = (synthesis / float(G * G * G)).astype(BF16)
    field = jnp.einsum(
        "rwax,abcwe->xerbc", synthesis, filtered, preferred_element_type=F32
    ).astype(BF16)
    field = field.reshape(slabs, planes * C, rows)

    partial = pl.pallas_call(
        functools.partial(inverse_kernel, planes=planes),
        out_shape=jax.ShapeDtypeStruct((slabs, C, slots), BF16),
        grid_spec=pltpu.PrefetchScalarGridSpec(
            num_scalar_prefetch=1,
            grid=(slabs,),
            in_specs=[region_block(16), region_block(rows), whole((slabs, planes * C, rows))],
            out_specs=region_block(C),
        ),
        compiler_params=params(),
        name="inverse",
    )(slab_ids, all_meta, wave, field)
    spectral = lax.psum_scatter(partial, "slab", scatter_dimension=0, tiled=False)

    cell_lifted = pl.pallas_call(
        cell_kernel,
        out_shape=jax.ShapeDtypeStruct((C, slots), F32),
        in_specs=[SMEM, SMEM, VMEM, VMEM, VMEM, VMEM],
        out_specs=VMEM,
        compiler_params=params(),
        name="cells",
    )(slab_ids, own_slab, all_lifted, share, key, own_key)

    out = pl.pallas_call(
        decode_kernel,
        out_shape=jax.ShapeDtypeStruct((C, points), BF16),
        in_specs=[VMEM] * 6,
        out_specs=VMEM,
        compiler_params=params(),
        name="decode",
    )(spectral, cell_lifted, meta, point_ids, skip_weight, proj_weight)
    return out.T


def solution(mesh):
    in_specs = (
        P(("groups", "slab"), None),
        P(None, ("groups", "slab")),
        P(("groups", "slab"), None, None),
        P(("groups", "slab"), None, None),
        P(),
        P(None, None, "slab", None, None, None),
        P(),
        P(),
    )
    out_specs = P(("groups", "slab"), None)
    return jax.shard_map(shards, mesh=mesh, in_specs=in_specs, out_specs=out_specs, check_vma=False)
```

```python
import functools

import jax
import jax.numpy as jnp
import numpy as np
from jax import lax
from jax.experimental import pallas as pl
from jax.experimental.pallas import tpu as pltpu
from jax.sharding import PartitionSpec as P

G = 128
C = 64
M = 32
RADIUS = 2
LISTS = 5
CAP = 256
SIDE = 4
VMEM_LIMIT = 48 * 1024 * 1024
F32 = jnp.float32
BF16 = jnp.bfloat16


def params():
    return pltpu.CompilerParams(vmem_limit_bytes=VMEM_LIMIT)


def frequencies(count, first=0):
    k = first + jnp.arange(count)
    return jnp.where(k < M // 2, k, k - M)


def waves(frequency, length):
    phase = (frequency[:, None] * jnp.arange(length)[None, :]) % length
    angle = (2.0 * jnp.pi / length) * phase.astype(F32)
    return jnp.cos(angle), jnp.sin(angle)


def nt_dot(left, right):
    return lax.dot_general(left, right, (((1,), (1,)), ((), ())), preferred_element_type=F32)


def dot(left, right):
    return jnp.dot(left, right, preferred_element_type=F32)


def prep_kernel(feat_ref, pos_ref, point_ref, cell_ref, slab_ref, lift_ref, lifted_ref, meta_ref, planes):
    points = feat_ref.shape[1]
    pos = pos_ref[...]
    high = pos.astype(BF16)
    rest = pos - high.astype(F32)
    middle = rest.astype(BF16)
    low = (rest - middle.astype(F32)).astype(BF16)
    lift = lift_ref[...]
    feat = feat_ref[...]
    for k in range(LISTS):
        place = pl.ds(k * CAP, CAP)
        point = point_ref[k : k + 1, :]
        cell = cell_ref[k : k + 1, :]
        live = cell >= 0
        cell = jnp.maximum(cell, 0)
        rows = lax.broadcasted_iota(jnp.int32, (points, CAP), 0)
        hot = jnp.where(rows == point, 1.0, 0.0).astype(BF16)
        got = dot(feat, hot).astype(BF16)
        lifted_ref[:, place] = lax.dot_general(
            lift, got, (((0,), (0,)), ((), ())), preferred_element_type=F32
        ).astype(BF16)
        at = dot(high, hot) + dot(middle, hot) + dot(low, hot)
        x = cell // (G * G) + slab_ref[k : k + 1, :] * planes
        y = cell // G % G
        z = cell % G
        xf, yf, zf = x.astype(F32), y.astype(F32), z.astype(F32)
        distance = (
            (at[0:1] - (xf + 0.5)) ** 2 + (at[1:2] - (yf + 0.5)) ** 2 + (at[2:3] - (zf + 0.5)) ** 2
        )
        kernel = 1.0 / (1.0 + distance / float(RADIUS * RADIUS))
        weight = jnp.where(live, kernel, 0.0)
        meta_ref[:, place] = jnp.concatenate(
            [xf, yf, zf, weight, jnp.zeros((12, CAP), F32)], axis=0
        ).astype(BF16)


def places(slabs):
    return (slabs // 4, 2) if slabs <= 16 else (slabs // 2, 1)


def peers(depth, width):
    me = lax.axis_index("slab")
    core, y, z = me % 2, (me // 2) % width, me // (2 * width)

    def at(z, y, core):
        return (z * width + y) * 2 + core

    return at, z, y, core


def greet(others):
    barrier = pltpu.get_barrier_semaphore()
    for other in others:
        pl.semaphore_signal(
            barrier, inc=1, device_id={"slab": other}, device_id_type=pl.DeviceIdType.MESH
        )
    pl.semaphore_wait(barrier, len(others))


def remote(source, target, send_sem, recv_sem, other):
    return pltpu.make_async_remote_copy(
        src_ref=source,
        dst_ref=target,
        send_sem=send_sem,
        recv_sem=recv_sem,
        device_id={"slab": other},
        device_id_type=pl.DeviceIdType.MESH,
    )


def gather_kernel(source_ref, out_ref, send_sem, recv_sem, own_sem, depth, width):
    at, z, y, core = peers(depth, width)
    ahead = [at((z + d) % depth, y, core) for d in range(1, depth)]
    beside = at(z, (y + 1) % width, core)
    twin = at(z, y, 1 - core)
    greet(ahead + ([beside] if width > 1 else []) + [twin])
    me = at(z, y, core)
    own = pltpu.make_async_copy(source_ref, out_ref.at[me], own_sem)
    own.start()
    sent = []

    def send(source, block, other):
        copy = remote(source, out_ref.at[block], send_sem.at[len(sent)], recv_sem.at[block], other)
        copy.start()
        sent.append(copy)

    def arrived(block):
        remote(source_ref, out_ref.at[block], send_sem.at[0], recv_sem.at[block], twin).wait_recv()

    for other in ahead:
        send(source_ref, me, other)
    if width > 1:
        send(source_ref, me, beside)
    send(source_ref, me, twin)
    for d in range(1, depth):
        block = at((z + depth - d) % depth, y, core)
        arrived(block)
        if width > 1:
            send(out_ref.at[block], block, beside)
        send(out_ref.at[block], block, twin)
    if width > 1:
        for d in range(depth):
            block = at((z + depth - d) % depth, 1 - y, core)
            arrived(block)
            send(out_ref.at[block], block, twin)
    for d in range(depth):
        for w in range(width):
            arrived(at((z + depth - d) % depth, (y + w) % width, 1 - core))
    own.wait()
    for copy in sent:
        copy.wait_send()


def gather(block, slabs, collective_id, name):
    depth, width = places(slabs)
    return pl.pallas_call(
        functools.partial(gather_kernel, depth=depth, width=width),
        out_shape=jax.ShapeDtypeStruct((slabs,) + block.shape, block.dtype),
        in_specs=[pl.BlockSpec(memory_space=pl.ANY)],
        out_specs=pl.BlockSpec(memory_space=pl.ANY),
        scratch_shapes=[
            pltpu.SemaphoreType.DMA((slabs,)),
            pltpu.SemaphoreType.DMA((slabs,)),
            pltpu.SemaphoreType.DMA,
        ],
        compiler_params=pltpu.CompilerParams(collective_id=collective_id, has_side_effects=True),
        name=name,
    )(block)


def scatter_kernel(
    blocks_ref, out_ref, from_core, from_y, from_z, to_y, to_z,
    core_send, core_recv, y_send, y_recv, z_send, z_recv, depth, width,
):
    at, z, y, core = peers(depth, width)
    ahead = [at((z + d) % depth, y, core) for d in range(1, depth)]
    beside = at(z, (y + 1) % width, core)
    twin = at(z, y, 1 - core)
    greet(ahead + ([beside] if width > 1 else []) + [twin])
    order = list(range(1, depth)) + [0]
    core_copies, y_copies, z_copies = {}, {}, {}
    for d in order:
        for w in reversed(range(width)):
            slot = d * width + w
            target = at((z + d) % depth, (y + w) % width, 1 - core)
            core_copies[slot] = remote(
                blocks_ref.at[target], from_core.at[slot], core_send.at[slot], core_recv.at[slot], twin
            )
            core_copies[slot].start()

    def pair(d, w):
        slot = d * width + w
        core_copies[slot].wait_recv()
        own = blocks_ref[at((z + d) % depth, (y + w) % width, core)].astype(F32)
        return own + from_core[slot].astype(F32)

    if width > 1:
        for d in order:
            to_y[d] = pair(d, 1).astype(BF16)
            y_copies[d] = remote(to_y.at[d], from_y.at[d], y_send.at[d], y_recv.at[d], beside)
            y_copies[d].start()
    for d in order:
        total = pair(d, 0)
        if width > 1:
            y_copies[d].wait_recv()
            total += from_y[d].astype(F32)
        if d > 0:
            to_z[d] = total.astype(BF16)
            z_copies[d] = remote(
                to_z.at[d], from_z.at[d], z_send.at[d], z_recv.at[d], ahead[d - 1]
            )
            z_copies[d].start()
        else:
            out_ref[...] = total
    for d in range(1, depth):
        z_copies[d].wait_recv()
        out_ref[...] += from_z[d].astype(F32)
    for copies in (core_copies, y_copies, z_copies):
        for copy in copies.values():
            copy.wait_send()


def scatter(blocks, slabs, collective_id, name):
    depth, width = places(slabs)
    shape = blocks.shape[1:]
    return pl.pallas_call(
        functools.partial(scatter_kernel, depth=depth, width=width),
        out_shape=jax.ShapeDtypeStruct(shape, F32),
        in_specs=[VMEM],
        out_specs=VMEM,
        scratch_shapes=[
            pltpu.VMEM((depth * width,) + shape, BF16),
            *[pltpu.VMEM((depth,) + shape, BF16)] * 4,
            *[pltpu.SemaphoreType.DMA((depth * width,))] * 2,
            *[pltpu.SemaphoreType.DMA((depth,))] * 4,
        ],
        compiler_params=pltpu.CompilerParams(
            collective_id=collective_id, has_side_effects=True, vmem_limit_bytes=VMEM_LIMIT
        ),
        name=name,
    )(blocks)


def share_kernel(slab_ref, own_slab_ref, key_ref, weight_ref, own_key_ref, own_meta_ref, lifted_ref, term_ref, bucket, count):
    lists = key_ref.shape[0]
    own = [own_slab_ref[k] for k in range(LISTS)]

    def fill(i, counts):
        s = slab_ref[i]
        for k in range(LISTS):
            bucket[k * lists + counts[k]] = i
        return tuple(n + (s == o).astype(jnp.int32) for n, o in zip(counts, own))

    counts = lax.fori_loop(0, lists, fill, (jnp.int32(0),) * LISTS)
    for k in range(LISTS):
        count[k] = counts[k]
        place = pl.ds(k * CAP, CAP)
        own_key = own_key_ref[k : k + 1, :]

        def add(p, total):
            i = bucket[k * lists + p]
            both = jnp.concatenate([key_ref[i], weight_ref[i], jnp.zeros((6, CAP), F32)], axis=0)
            turned = both.T
            terms = jnp.where(turned[:, 0:1] == own_key, turned[:, 1:2], 0.0)
            return total + jnp.sum(terms, axis=0, keepdims=True)

        total = lax.fori_loop(0, counts[k], add, jnp.zeros((1, CAP), F32))
        weight = own_meta_ref[:, place].astype(F32)[3:4]
        scaled = lifted_ref[:, place].astype(F32) * (weight / (1.0 + total))
        term_ref[:, place] = scaled.astype(BF16)


def forward_kernel(slab_ref, lifted_ref, meta_ref, tab_y_ref, tab_z_ref, tab_x_ref, modes_ref, wave_ref, total, lines, planes):
    region = pl.program_id(0)
    rows = wave_ref.shape[1]

    @pl.when(region == 0)
    def _():
        total[...] = jnp.zeros_like(total)

    for k in range(LISTS):
        place = pl.ds(k * CAP, CAP)
        slab = slab_ref[region * LISTS + k]
        meta = meta_ref[0, :, place].astype(F32)
        line = lax.broadcasted_iota(jnp.int32, (G, CAP), 0).astype(F32)
        hot_y = jnp.where(line == meta[1:2], 1.0, 0.0).astype(BF16)
        hot_z = jnp.where(line == meta[2:3], 1.0, 0.0).astype(BF16)
        along_y = dot(tab_y_ref[...], hot_y)
        along_z = dot(tab_z_ref[...], hot_z)
        wave = along_y[:rows] * along_z[:rows] + along_y[rows:] * along_z[rows:]
        wave = wave.astype(BF16)
        wave_ref[0, :, place] = wave
        scaled = lifted_ref[0, :, place]
        local = meta[0:1] - (slab * planes).astype(F32)
        parts = [
            scaled * jnp.where(local == float(p), 1.0, 0.0).astype(BF16) for p in range(planes)
        ]
        height = planes * C
        at = pl.ds(pl.multiple_of(slab * height, height), height)
        total[at, :] += nt_dot(jnp.concatenate(parts, axis=0), wave)

    @pl.when(region == pl.num_programs(0) - 1)
    def _():
        half = rows // 2
        sign = jnp.where(lax.broadcasted_iota(jnp.int32, (M, rows), 1) < half, 1.0, -1.0)

        def along_x(d, _):
            line = total[pl.ds(d, G, stride=C), :].astype(BF16)
            both = dot(tab_x_ref[...], line)
            turned = jnp.concatenate([both[M:, half:], both[M:, :half]], axis=1)
            lines[pl.ds(pl.multiple_of(d * M, M), M), :] = both[:M] + sign * turned
            return 0

        lax.fori_loop(0, C, along_x, 0, unroll=16)
        for a in range(M):
            modes_ref[a] = lines[pl.ds(a, C, stride=M), :].astype(BF16)


def mix_kernel(modes_ref, weight_ref, spread_ref, collect_ref, out_ref, products):
    columns, own_modes = weight_ref.shape[1], weight_ref.shape[2]
    depth, height = own_modes * 2 * C, own_modes * 2 * SIDE
    modes = modes_ref[0]
    sides = [nt_dot(spread_ref[i], modes) for i in range(spread_ref.shape[0])]
    left = jnp.concatenate(sides, axis=1)
    for g in range(columns // SIDE):
        weights = [weight_ref[0, SIDE * g + i].reshape(depth, C) for i in range(SIDE)]
        rows = slice(height * g, height * (g + 1))
        products[rows, :] = dot(left[rows].astype(BF16), jnp.concatenate(weights, axis=1))
    turned = lax.dot_general(
        products[...].astype(BF16),
        collect_ref[...],
        (((0,), (0,)), ((), ())),
        preferred_element_type=F32,
    )
    lane = lax.broadcasted_iota(jnp.int32, (C, turned.shape[1]), 1)
    side = lane // own_modes % SIDE
    total = turned[:C]
    for i in range(1, SIDE):
        total = jnp.where(side == i, turned[i * C : (i + 1) * C], total)
    out_ref[0] = total


def inverse_kernel(slab_ref, meta_ref, wave_ref, mixed_ref, tab_x_ref, out_ref, lines, field, planes):
    region = pl.program_id(0)
    rows = wave_ref.shape[1]
    height = planes * C

    @pl.when(region == 0)
    def _():
        half = rows // 2
        sign = jnp.where(lax.broadcasted_iota(jnp.int32, (M, rows), 1) < half, -1.0, 1.0)

        def along_x(e, _):
            line = mixed_ref[pl.ds(e, M, stride=C), :]
            turned = sign * jnp.concatenate([line[:, half:], line[:, :half]], axis=1)
            both = jnp.concatenate([line, turned], axis=0).astype(BF16)
            lines[pl.ds(e, G, stride=C), :] = dot(tab_x_ref[...], both)
            return 0

        lax.fori_loop(0, C, along_x, 0, unroll=16)
        field[...] = lines[...].astype(BF16)

    for k in range(LISTS):
        place = pl.ds(k * CAP, CAP)
        slab = slab_ref[region * LISTS + k]
        local = meta_ref[0, :, place].astype(F32)[0:1] - (slab * planes).astype(F32)
        at = pl.ds(pl.multiple_of(slab * height, height), height)
        values = dot(field[at, :], wave_ref[0, :, place])
        total = jnp.zeros((C, CAP), F32)
        for p in range(planes):
            total += jnp.where(local == float(p), values[p * C : (p + 1) * C], 0.0)
        out_ref[0, :, place] = total.astype(BF16)


def cell_kernel(bucket, count, lifted_ref, key_ref, own_key_ref, out_ref):
    lists = key_ref.shape[0]
    for k in range(LISTS):
        own = own_key_ref[k : k + 1, :]
        turned = jnp.broadcast_to(own, (8, CAP)).T[:, 0:1]

        def add(p, total):
            i = bucket[k * lists + p]
            same = jnp.where(turned == key_ref[i], 1.0, 0.0).astype(BF16)
            slots = pl.ds(pl.multiple_of((i % LISTS) * CAP, CAP), CAP)
            return total + nt_dot(lifted_ref[i // LISTS, :, slots], same)

        out_ref[:, pl.ds(k * CAP, CAP)] = lax.fori_loop(
            0, count[k], add, jnp.zeros((C, CAP), F32)
        )


def decode_kernel(spectral_ref, cell_ref, meta_ref, point_ref, skip_ref, proj_ref, out_ref):
    points = out_ref.shape[1]
    total = jnp.zeros((C + 16, points), F32)
    for k in range(LISTS):
        place = pl.ds(k * CAP, CAP)
        skip = lax.dot_general(
            skip_ref[...],
            cell_ref[:, place].astype(BF16),
            (((0,), (0,)), ((), ())),
            preferred_element_type=F32,
        )
        u = spectral_ref[:, place].astype(F32) + skip
        hidden = 0.5 * u * (1.0 + jnp.tanh(0.7978845608028654 * (u + 0.044715 * u * u * u)))
        hidden = jnp.concatenate([hidden, jnp.ones((16, CAP), F32)], axis=0).astype(BF16)
        weight = meta_ref[:, place].astype(F32)[3:4]
        rows = lax.broadcasted_iota(jnp.int32, (points, CAP), 0)
        hot = jnp.where(rows == point_ref[k : k + 1, :], weight, 0.0).astype(BF16)
        total += nt_dot(hidden, hot)
    mean = (total[:C] / (1.0 + total[C : C + 1])).astype(BF16)
    out_ref[...] = lax.dot_general(
        proj_ref[...], mean, (((0,), (0,)), ((), ())), preferred_element_type=F32
    ).astype(BF16)


def selections(own_modes):
    spread = np.zeros((own_modes, 2, M, 2 * own_modes, 2, M, own_modes), np.float32)
    collect = np.zeros((M, 2 * own_modes, 2, M, own_modes), np.float32)
    for b in range(M):
        for c in range(own_modes):
            for w in range(2):
                collect[b, 2 * c + w, w, b, c] = 1.0
                for s in range(2):
                    spread[c, s, b, 2 * c + w, s ^ w, b, c] = -1.0 if s > w else 1.0
    rows = 2 * M * own_modes
    return (
        jnp.asarray(spread.reshape(2 * own_modes, rows, rows), BF16),
        jnp.asarray(collect.reshape(rows, rows), BF16),
    )


def compact(lists, live):
    rank = jnp.cumsum(live.astype(jnp.int32)) - 1
    hot = live[None, :] & (rank[None, :] == jnp.arange(LISTS)[:, None])
    return jnp.sum(jnp.where(hot[:, :, None], lists[None] + 1, 0), axis=1) - 1, hot


def pad8(array):
    return jnp.concatenate([array, jnp.full((8 - LISTS, array.shape[1]), -1, array.dtype)], axis=0)


VMEM = pl.BlockSpec(memory_space=pltpu.VMEM)
SMEM = pl.BlockSpec(memory_space=pltpu.SMEM)


def shards(
    point_feat,
    point_pos,
    pair_point,
    pair_cell,
    lift_weight,
    spectral_weight,
    skip_weight,
    proj_weight,
):
    slabs = lax.axis_size("slab")
    me = lax.axis_index("slab")
    planes = G // slabs
    own_modes = spectral_weight.shape[2]
    rows = 2 * M * own_modes
    slots = LISTS * CAP
    lists = slabs * LISTS
    points = point_feat.shape[0]

    live = pair_cell[0, :, 0] >= 0
    cells, hot = compact(pair_cell[0], live)
    point_ids, _ = compact(pair_point[0], live)
    own_slab = jnp.sum(jnp.where(hot, jnp.arange(slabs)[None, :], 0), axis=1).astype(jnp.int32)
    cells, point_ids = pad8(cells), pad8(point_ids)
    slab_rows = jnp.broadcast_to(own_slab[:, None], (LISTS, CAP))

    lifted, meta = pl.pallas_call(
        functools.partial(prep_kernel, planes=planes),
        out_shape=(
            jax.ShapeDtypeStruct((C, slots), BF16),
            jax.ShapeDtypeStruct((16, slots), BF16),
        ),
        in_specs=[VMEM] * 6,
        out_specs=(VMEM, VMEM),
        compiler_params=params(),
        name="prep",
    )(point_feat.T, point_pos, point_ids, cells, pad8(slab_rows), lift_weight)

    all_meta = gather(meta, slabs, 0, "gather_meta")

    def keys(values):
        values = values.astype(F32)
        return (values[..., 0, :] * G + values[..., 1, :]) * G + values[..., 2, :]

    key = keys(all_meta).reshape(lists, 1, CAP)
    weight = all_meta[:, 3].astype(F32).reshape(lists, 1, CAP)
    slab_ids = (all_meta[:, 0, ::CAP].astype(jnp.int32) // planes).reshape(lists)
    own_key = pad8(keys(meta).reshape(LISTS, CAP))

    terms, bucket, count = pl.pallas_call(
        share_kernel,
        out_shape=(
            jax.ShapeDtypeStruct((C, slots), BF16),
            jax.ShapeDtypeStruct(((LISTS + 1) * lists,), jnp.int32),
            jax.ShapeDtypeStruct((LISTS,), jnp.int32),
        ),
        in_specs=[SMEM, SMEM, VMEM, VMEM, VMEM, VMEM, VMEM],
        out_specs=(VMEM, SMEM, SMEM),
        compiler_params=params(),
        name="share",
    )(slab_ids, own_slab, key, weight, own_key, meta, lifted)
    all_terms = gather(terms, slabs, 1, "gather_terms")

    cos_y, sin_y = waves(frequencies(M), G)
    cos_z, sin_z = waves(frequencies(own_modes, me * own_modes), G)
    cos_b, sin_b = jnp.repeat(cos_y, own_modes, 0), jnp.repeat(sin_y, own_modes, 0)
    cos_c, sin_c = jnp.tile(cos_z, (2 * M, 1)), jnp.tile(sin_z, (2 * M, 1))
    tab_y = jnp.concatenate([cos_b, -sin_b, -sin_b, -cos_b], 0).astype(BF16)
    tab_z = jnp.concatenate([cos_c, sin_c], 0).astype(BF16)

    def region_block(height):
        return pl.BlockSpec((1, height, slots), lambda r, ids: (r, 0, 0))

    def whole(shape):
        return pl.BlockSpec(shape, lambda r, ids: (0,) * len(shape))

    tab_x = jnp.concatenate([cos_y, sin_y], 0)
    modes, wave = pl.pallas_call(
        functools.partial(forward_kernel, planes=planes),
        out_shape=(
            jax.ShapeDtypeStruct((M, C, rows), BF16),
            jax.ShapeDtypeStruct((slabs, rows, slots), BF16),
        ),
        grid_spec=pltpu.PrefetchScalarGridSpec(
            num_scalar_prefetch=1,
            grid=(slabs,),
            in_specs=[
                region_block(C),
                region_block(16),
                whole((2 * rows, G)),
                whole((2 * rows, G)),
                whole((2 * M, G)),
            ],
            out_specs=(whole((M, C, rows)), region_block(rows)),
            scratch_shapes=[pltpu.VMEM((G * C, rows), F32), pltpu.VMEM((C * M, rows), F32)],
        ),
        compiler_params=params(),
        name="forward",
    )(slab_ids, all_terms, all_meta, tab_y, tab_z, tab_x.astype(BF16))

    spread, collect = selections(own_modes)
    mixed = pl.pallas_call(
        mix_kernel,
        out_shape=jax.ShapeDtypeStruct((M, C, rows), F32),
        grid=(M,),
        in_specs=[
            pl.BlockSpec((1, C, rows), lambda a: (a, 0, 0)),
            pl.BlockSpec((1, M, own_modes, 2, C, C), lambda a: (a, 0, 0, 0, 0, 0)),
            pl.BlockSpec(spread.shape, lambda a: (0, 0, 0)),
            pl.BlockSpec(collect.shape, lambda a: (0, 0)),
        ],
        out_specs=pl.BlockSpec((1, C, rows), lambda a: (a, 0, 0)),
        scratch_shapes=[pltpu.VMEM((2 * own_modes * M, SIDE * C), F32)],
        compiler_params=params(),
        name="mix",
    )(modes, spectral_weight, spread, collect)

    partial = pl.pallas_call(
        functools.partial(inverse_kernel, planes=planes),
        out_shape=jax.ShapeDtypeStruct((slabs, C, slots), BF16),
        grid_spec=pltpu.PrefetchScalarGridSpec(
            num_scalar_prefetch=1,
            grid=(slabs,),
            in_specs=[
                region_block(16),
                region_block(rows),
                whole((M * C, rows)),
                whole((G, 2 * M)),
            ],
            out_specs=region_block(C),
            scratch_shapes=[pltpu.VMEM((G * C, rows), F32), pltpu.VMEM((G * C, rows), BF16)],
        ),
        compiler_params=params(),
        name="inverse",
    )(slab_ids, all_meta, wave, mixed.reshape(M * C, rows), (tab_x.T / float(G * G * G)).astype(BF16))
    spectral = scatter(partial, slabs, 2, "scatter")

    cell_lifted = pl.pallas_call(
        cell_kernel,
        out_shape=jax.ShapeDtypeStruct((C, slots), F32),
        in_specs=[SMEM, SMEM, VMEM, VMEM, VMEM],
        out_specs=VMEM,
        compiler_params=params(),
        name="cells",
    )(bucket, count, all_terms, key, own_key)

    out = pl.pallas_call(
        decode_kernel,
        out_shape=jax.ShapeDtypeStruct((C, points), BF16),
        in_specs=[VMEM] * 6,
        out_specs=VMEM,
        compiler_params=params(),
        name="decode",
    )(spectral, cell_lifted, meta, point_ids, skip_weight, proj_weight)
    return out.T


def solution(mesh):
    in_specs = (
        P(("groups", "slab"), None),
        P(None, ("groups", "slab")),
        P(("groups", "slab"), None, None),
        P(("groups", "slab"), None, None),
        P(),
        P(None, None, "slab", None, None, None),
        P(),
        P(),
    )
    out_specs = P(("groups", "slab"), None)
    return jax.shard_map(shards, mesh=mesh, in_specs=in_specs, out_specs=out_specs, check_vma=False)
```

```python
import functools

import jax
import jax.numpy as jnp
import numpy as np
from jax import lax
from jax.experimental import pallas as pl
from jax.experimental.pallas import tpu as pltpu
from jax.sharding import PartitionSpec as P

G = 128
C = 64
M = 32
RADIUS = 2
LISTS = 5
CAP = 256
HELD = 20
STEP = 4
SIDE = 4
VMEM_LIMIT = 32 * 1024 * 1024
VMEM_MOST = 58 * 1024 * 1024
F32 = jnp.float32
BF16 = jnp.bfloat16


def params(limit=VMEM_LIMIT):
    return pltpu.CompilerParams(vmem_limit_bytes=limit)


def frequencies(count, first=0):
    k = first + jnp.arange(count)
    return jnp.where(k < M // 2, k, k - M)


def waves(frequency, length):
    phase = (frequency[:, None] * jnp.arange(length)[None, :]) % length
    angle = (2.0 * jnp.pi / length) * phase.astype(F32)
    return jnp.cos(angle), jnp.sin(angle)


def nt_dot(left, right):
    return lax.dot_general(left, right, (((1,), (1,)), ((), ())), preferred_element_type=F32)


def dot(left, right):
    return jnp.dot(left, right, preferred_element_type=F32)


def prep_kernel(feat_ref, pos_ref, point_ref, cell_ref, slab_ref, lift_ref, lifted_ref, meta_ref, planes):
    points = feat_ref.shape[1]
    pos = pos_ref[...]
    high = pos.astype(BF16)
    rest = pos - high.astype(F32)
    middle = rest.astype(BF16)
    low = (rest - middle.astype(F32)).astype(BF16)
    lift = lift_ref[...]
    feat = feat_ref[...]
    for k in range(LISTS):
        place = pl.ds(k * CAP, CAP)
        point = point_ref[k : k + 1, :]
        cell = cell_ref[k : k + 1, :]
        live = cell >= 0
        cell = jnp.maximum(cell, 0)
        rows = lax.broadcasted_iota(jnp.int32, (points, CAP), 0)
        hot = jnp.where(rows == point, 1.0, 0.0).astype(BF16)
        got = dot(feat, hot).astype(BF16)
        lifted_ref[:, place] = lax.dot_general(
            lift, got, (((0,), (0,)), ((), ())), preferred_element_type=F32
        ).astype(BF16)
        at = dot(high, hot) + dot(middle, hot) + dot(low, hot)
        x = cell // (G * G) + slab_ref[k : k + 1, :] * planes
        y = cell // G % G
        z = cell % G
        xf, yf, zf = x.astype(F32), y.astype(F32), z.astype(F32)
        distance = (
            (at[0:1] - (xf + 0.5)) ** 2 + (at[1:2] - (yf + 0.5)) ** 2 + (at[2:3] - (zf + 0.5)) ** 2
        )
        kernel = 1.0 / (1.0 + distance / float(RADIUS * RADIUS))
        weight = jnp.where(live, kernel, 0.0)
        meta_ref[:, place] = jnp.concatenate(
            [xf, yf, zf, weight, jnp.zeros((12, CAP), F32)], axis=0
        ).astype(BF16)


def places(slabs):
    return (slabs // 4, 2) if slabs <= 16 else (slabs // 2, 1)


def peers(depth, width):
    me = lax.axis_index("slab")
    core, y, z = me % 2, (me // 2) % width, me // (2 * width)

    def at(z, y, core):
        return (z * width + y) * 2 + core

    return at, z, y, core


def greet(others):
    barrier = pltpu.get_barrier_semaphore()
    for other in others:
        pl.semaphore_signal(
            barrier, inc=1, device_id={"slab": other}, device_id_type=pl.DeviceIdType.MESH
        )
    pl.semaphore_wait(barrier, len(others))


def remote(source, target, send_sem, recv_sem, other):
    return pltpu.make_async_remote_copy(
        src_ref=source,
        dst_ref=target,
        send_sem=send_sem,
        recv_sem=recv_sem,
        device_id={"slab": other},
        device_id_type=pl.DeviceIdType.MESH,
    )


def gather_kernel(source_ref, out_ref, send_sem, recv_sem, own_sem, depth, width):
    at, z, y, core = peers(depth, width)
    ahead = [at((z + d) % depth, y, core) for d in range(1, depth)]
    beside = at(z, (y + 1) % width, core)
    twin = at(z, y, 1 - core)
    greet(ahead + ([beside] if width > 1 else []) + [twin])
    me = at(z, y, core)
    own = pltpu.make_async_copy(source_ref, out_ref.at[me], own_sem)
    own.start()
    sent = []

    def send(source, block, other):
        copy = remote(source, out_ref.at[block], send_sem.at[len(sent)], recv_sem.at[block], other)
        copy.start()
        sent.append(copy)

    def arrived(block):
        remote(source_ref, out_ref.at[block], send_sem.at[0], recv_sem.at[block], twin).wait_recv()

    for other in ahead:
        send(source_ref, me, other)
    if width > 1:
        send(source_ref, me, beside)
    send(source_ref, me, twin)
    for d in range(1, depth):
        block = at((z + depth - d) % depth, y, core)
        arrived(block)
        if width > 1:
            send(out_ref.at[block], block, beside)
        send(out_ref.at[block], block, twin)
    if width > 1:
        for d in range(depth):
            block = at((z + depth - d) % depth, 1 - y, core)
            arrived(block)
            send(out_ref.at[block], block, twin)
    for d in range(depth):
        for w in range(width):
            arrived(at((z + depth - d) % depth, (y + w) % width, 1 - core))
    own.wait()
    for copy in sent:
        copy.wait_send()


def gather(block, slabs, collective_id, name):
    depth, width = places(slabs)
    return pl.pallas_call(
        functools.partial(gather_kernel, depth=depth, width=width),
        out_shape=jax.ShapeDtypeStruct((slabs,) + block.shape, block.dtype),
        in_specs=[pl.BlockSpec(memory_space=pl.ANY)],
        out_specs=pl.BlockSpec(memory_space=pl.ANY),
        scratch_shapes=[
            pltpu.SemaphoreType.DMA((slabs,)),
            pltpu.SemaphoreType.DMA((slabs,)),
            pltpu.SemaphoreType.DMA,
        ],
        compiler_params=pltpu.CompilerParams(collective_id=collective_id, has_side_effects=True),
        name=name,
    )(block)


def scatter_kernel(
    blocks_ref, out_ref, from_core, from_y, from_z, to_y, to_z,
    core_send, core_recv, y_send, y_recv, z_send, z_recv, depth, width,
):
    at, z, y, core = peers(depth, width)
    ahead = [at((z + d) % depth, y, core) for d in range(1, depth)]
    beside = at(z, (y + 1) % width, core)
    twin = at(z, y, 1 - core)
    greet(ahead + ([beside] if width > 1 else []) + [twin])
    order = list(range(1, depth)) + [0]
    core_copies, y_copies, z_copies = {}, {}, {}
    for d in order:
        for w in reversed(range(width)):
            slot = d * width + w
            target = at((z + d) % depth, (y + w) % width, 1 - core)
            core_copies[slot] = remote(
                blocks_ref.at[target], from_core.at[slot], core_send.at[slot], core_recv.at[slot], twin
            )
            core_copies[slot].start()

    def pair(d, w):
        slot = d * width + w
        core_copies[slot].wait_recv()
        own = blocks_ref[at((z + d) % depth, (y + w) % width, core)].astype(F32)
        return own + from_core[slot].astype(F32)

    if width > 1:
        for d in order:
            to_y[d] = pair(d, 1).astype(BF16)
            y_copies[d] = remote(to_y.at[d], from_y.at[d], y_send.at[d], y_recv.at[d], beside)
            y_copies[d].start()
    for d in order:
        total = pair(d, 0)
        if width > 1:
            y_copies[d].wait_recv()
            total += from_y[d].astype(F32)
        if d > 0:
            to_z[d] = total.astype(BF16)
            z_copies[d] = remote(
                to_z.at[d], from_z.at[d], z_send.at[d], z_recv.at[d], ahead[d - 1]
            )
            z_copies[d].start()
        else:
            out_ref[...] = total
    for d in range(1, depth):
        z_copies[d].wait_recv()
        out_ref[...] += from_z[d].astype(F32)
    for copies in (core_copies, y_copies, z_copies):
        for copy in copies.values():
            copy.wait_send()


def scatter(blocks, slabs, collective_id, name):
    depth, width = places(slabs)
    shape = blocks.shape[1:]
    return pl.pallas_call(
        functools.partial(scatter_kernel, depth=depth, width=width),
        out_shape=jax.ShapeDtypeStruct(shape, F32),
        in_specs=[VMEM],
        out_specs=VMEM,
        scratch_shapes=[
            pltpu.VMEM((depth * width,) + shape, BF16),
            *[pltpu.VMEM((depth,) + shape, BF16)] * 4,
            *[pltpu.SemaphoreType.DMA((depth * width,))] * 2,
            *[pltpu.SemaphoreType.DMA((depth,))] * 4,
        ],
        compiler_params=pltpu.CompilerParams(
            collective_id=collective_id, has_side_effects=True, vmem_limit_bytes=VMEM_LIMIT
        ),
        name=name,
    )(blocks)


def share_kernel(slab_ref, own_slab_ref, key_ref, weight_ref, own_key_ref, own_meta_ref, lifted_ref, term_ref, bucket, count):
    lists = key_ref.shape[0]
    own = [own_slab_ref[k] for k in range(LISTS)]

    def fill(i, counts):
        s = slab_ref[i]
        for k in range(LISTS):
            bucket[k * lists + counts[k]] = i
        return tuple(n + (s == o).astype(jnp.int32) for n, o in zip(counts, own))

    counts = lax.fori_loop(0, lists, fill, (jnp.int32(0),) * LISTS)
    for k in range(LISTS):
        count[k] = counts[k]
    own_keys = [own_key_ref[k : k + 1, :] for k in range(LISTS)]

    def add(p, totals):
        added = []
        for k in range(LISTS):
            valid = p < counts[k]
            i = jnp.where(valid, bucket[k * lists + p], 0)
            weight = jnp.where(valid, weight_ref[i], 0.0)
            both = jnp.concatenate([key_ref[i], weight, jnp.zeros((6, CAP), F32)], axis=0)
            turned = both.T
            terms = jnp.where(turned[:, 0:1] == own_keys[k], turned[:, 1:2], 0.0)
            added.append(totals[k] + jnp.sum(terms, axis=0, keepdims=True))
        return tuple(added)

    longest = functools.reduce(jnp.maximum, counts)
    totals = lax.fori_loop(0, longest, add, (jnp.zeros((1, CAP), F32),) * LISTS)
    for k in range(LISTS):
        place = pl.ds(k * CAP, CAP)
        weight = own_meta_ref[:, place].astype(F32)[3:4]
        scaled = lifted_ref[:, place].astype(F32) * (weight / (1.0 + totals[k]))
        term_ref[:, place] = scaled.astype(BF16)


def mix_modes(modes, weight_refs, spread_ref, collect_ref):
    columns, own_modes = weight_refs[0].shape[0], weight_refs[0].shape[1]
    depth, height = own_modes * 2 * C, own_modes * 2 * SIDE
    lefts = []
    for mode in modes:
        sides = [nt_dot(spread_ref[i], mode) for i in range(spread_ref.shape[0])]
        lefts.append(jnp.concatenate(sides, axis=1))
    products = []
    for left, weight_ref in zip(lefts, weight_refs):
        blocks = []
        for g in range(columns // SIDE):
            weights = [weight_ref[SIDE * g + i].reshape(depth, C) for i in range(SIDE)]
            rows = slice(height * g, height * (g + 1))
            blocks.append(dot(left[rows].astype(BF16), jnp.concatenate(weights, axis=1)))
        products.append(jnp.concatenate(blocks, axis=0).astype(BF16))
    outs = []
    for product in products:
        turned = lax.dot_general(
            product, collect_ref[...], (((0,), (0,)), ((), ())), preferred_element_type=F32
        )
        lane = lax.broadcasted_iota(jnp.int32, (C, turned.shape[1]), 1)
        side = lane // own_modes % SIDE
        total = turned[:C]
        for i in range(1, SIDE):
            total = jnp.where(side == i, turned[i * C : (i + 1) * C], total)
        outs.append(total)
    return outs


def forward_kernel(
    slab_ref, lifted_ref, meta_ref, tab_y_ref, tab_z_ref, tab_x_ref, spread_ref, collect_ref,
    weight_ref, out_ref, wave_ref, total, lines, modes, weights, weight_sem, planes,
):
    region = pl.program_id(0)
    rows = wave_ref.shape[1]
    held = weights.shape[0]

    def fetch(a, slot):
        return pltpu.make_async_copy(weight_ref.at[a], weights.at[slot], weight_sem.at[slot])

    @pl.when(region == 0)
    def _():
        for a in range(held):
            fetch(a, a).start()
        total[...] = jnp.zeros_like(total)

    for k in range(LISTS):
        place = pl.ds(k * CAP, CAP)
        slab = slab_ref[region * LISTS + k]
        meta = meta_ref[0, :, place].astype(F32)
        line = lax.broadcasted_iota(jnp.int32, (G, CAP), 0).astype(F32)
        hot_y = jnp.where(line == meta[1:2], 1.0, 0.0).astype(BF16)
        hot_z = jnp.where(line == meta[2:3], 1.0, 0.0).astype(BF16)
        along_y = dot(tab_y_ref[...], hot_y)
        along_z = dot(tab_z_ref[...], hot_z)
        wave = along_y[:rows] * along_z[:rows] + along_y[rows:] * along_z[rows:]
        wave = wave.astype(BF16)
        wave_ref[0, :, place] = wave
        scaled = lifted_ref[0, :, place]
        local = meta[0:1] - (slab * planes).astype(F32)
        parts = [
            scaled * jnp.where(local == float(p), 1.0, 0.0).astype(BF16) for p in range(planes)
        ]
        height = planes * C
        at = pl.ds(pl.multiple_of(slab * height, height), height)
        total[at, :] += nt_dot(jnp.concatenate(parts, axis=0), wave)

    @pl.when(region == pl.num_programs(0) - 1)
    def _():
        half = rows // 2
        sign = jnp.where(lax.broadcasted_iota(jnp.int32, (M, rows), 1) < half, 1.0, -1.0)

        def along_x(d, _):
            line = total[pl.ds(d, G, stride=C), :].astype(BF16)
            both = dot(tab_x_ref[...], line)
            turned = jnp.concatenate([both[M:, half:], both[M:, :half]], axis=1)
            lines[pl.ds(pl.multiple_of(d * M, M), M), :] = both[:M] + sign * turned
            return 0

        lax.fori_loop(0, C, along_x, 0, unroll=16)
        for a in range(M):
            modes[a] = lines[pl.ds(a, C, stride=M), :].astype(BF16)

        def mix(step, _):
            first = step * STEP
            places = [(first + i) % held for i in range(STEP)]
            for i in range(STEP):
                fetch(first + i, places[i]).wait()
            outs = mix_modes(
                [modes[first + i] for i in range(STEP)],
                [weights.at[place] for place in places],
                spread_ref,
                collect_ref,
            )
            for i in range(STEP):
                out_ref[first + i] = outs[i]

            @pl.when(first + held < M)
            def _():
                for i in range(STEP):
                    fetch(first + held + i, places[i]).start()

            return 0

        lax.fori_loop(0, M // STEP, mix, 0)


def inverse_kernel(slab_ref, meta_ref, wave_ref, mixed_ref, tab_x_ref, out_ref, lines, field, planes):
    region = pl.program_id(0)
    rows = wave_ref.shape[1]
    height = planes * C

    @pl.when(region == 0)
    def _():
        half = rows // 2
        sign = jnp.where(lax.broadcasted_iota(jnp.int32, (M, rows), 1) < half, -1.0, 1.0)

        def along_x(e, _):
            line = mixed_ref[pl.ds(e, M, stride=C), :]
            turned = sign * jnp.concatenate([line[:, half:], line[:, :half]], axis=1)
            both = jnp.concatenate([line, turned], axis=0).astype(BF16)
            lines[pl.ds(e, G, stride=C), :] = dot(tab_x_ref[...], both)
            return 0

        lax.fori_loop(0, C, along_x, 0, unroll=16)
        field[...] = lines[...].astype(BF16)

    for k in range(LISTS):
        place = pl.ds(k * CAP, CAP)
        slab = slab_ref[region * LISTS + k]
        local = meta_ref[0, :, place].astype(F32)[0:1] - (slab * planes).astype(F32)
        at = pl.ds(pl.multiple_of(slab * height, height), height)
        values = dot(field[at, :], wave_ref[0, :, place])
        total = jnp.zeros((C, CAP), F32)
        for p in range(planes):
            total += jnp.where(local == float(p), values[p * C : (p + 1) * C], 0.0)
        out_ref[0, :, place] = total.astype(BF16)


def cell_kernel(bucket, count, lifted_ref, key_ref, own_key_ref, out_ref):
    lists = key_ref.shape[0]
    counts = [count[k] for k in range(LISTS)]
    out_ref[...] = jnp.zeros_like(out_ref)
    turned = [
        jnp.broadcast_to(own_key_ref[k : k + 1, :], (8, CAP)).T[:, 0:1] for k in range(LISTS)
    ]

    def add(p, _):
        for k in range(LISTS):
            valid = p < counts[k]
            i = jnp.where(valid, bucket[k * lists + p], 0)
            key = jnp.where(valid, key_ref[i], -1.0)
            same = jnp.where(turned[k] == key, 1.0, 0.0).astype(BF16)
            slots = pl.ds(pl.multiple_of((i % LISTS) * CAP, CAP), CAP)
            out_ref[:, pl.ds(k * CAP, CAP)] += nt_dot(lifted_ref[i // LISTS, :, slots], same)
        return 0

    lax.fori_loop(0, functools.reduce(jnp.maximum, counts), add, 0)


def decode_kernel(spectral_ref, cell_ref, meta_ref, point_ref, skip_ref, proj_ref, out_ref):
    points = out_ref.shape[1]
    total = jnp.zeros((C + 16, points), F32)
    for k in range(LISTS):
        place = pl.ds(k * CAP, CAP)
        skip = lax.dot_general(
            skip_ref[...],
            cell_ref[:, place].astype(BF16),
            (((0,), (0,)), ((), ())),
            preferred_element_type=F32,
        )
        u = spectral_ref[:, place].astype(F32) + skip
        hidden = 0.5 * u * (1.0 + jnp.tanh(0.7978845608028654 * (u + 0.044715 * u * u * u)))
        hidden = jnp.concatenate([hidden, jnp.ones((16, CAP), F32)], axis=0).astype(BF16)
        weight = meta_ref[:, place].astype(F32)[3:4]
        rows = lax.broadcasted_iota(jnp.int32, (points, CAP), 0)
        hot = jnp.where(rows == point_ref[k : k + 1, :], weight, 0.0).astype(BF16)
        total += nt_dot(hidden, hot)
    mean = (total[:C] / (1.0 + total[C : C + 1])).astype(BF16)
    out_ref[...] = lax.dot_general(
        proj_ref[...], mean, (((0,), (0,)), ((), ())), preferred_element_type=F32
    ).astype(BF16)


def selections(own_modes):
    spread = np.zeros((own_modes, 2, M, 2 * own_modes, 2, M, own_modes), np.float32)
    collect = np.zeros((M, 2 * own_modes, 2, M, own_modes), np.float32)
    for b in range(M):
        for c in range(own_modes):
            for w in range(2):
                collect[b, 2 * c + w, w, b, c] = 1.0
                for s in range(2):
                    spread[c, s, b, 2 * c + w, s ^ w, b, c] = -1.0 if s > w else 1.0
    rows = 2 * M * own_modes
    return (
        jnp.asarray(spread.reshape(2 * own_modes, rows, rows), BF16),
        jnp.asarray(collect.reshape(rows, rows), BF16),
    )


def compact(lists, live):
    rank = jnp.cumsum(live.astype(jnp.int32)) - 1
    hot = live[None, :] & (rank[None, :] == jnp.arange(LISTS)[:, None])
    return jnp.sum(jnp.where(hot[:, :, None], lists[None] + 1, 0), axis=1) - 1, hot


def pad8(array):
    return jnp.concatenate([array, jnp.full((8 - LISTS, array.shape[1]), -1, array.dtype)], axis=0)


VMEM = pl.BlockSpec(memory_space=pltpu.VMEM)
SMEM = pl.BlockSpec(memory_space=pltpu.SMEM)


def shards(
    point_feat,
    point_pos,
    pair_point,
    pair_cell,
    lift_weight,
    spectral_weight,
    skip_weight,
    proj_weight,
):
    slabs = lax.axis_size("slab")
    me = lax.axis_index("slab")
    planes = G // slabs
    own_modes = spectral_weight.shape[2]
    rows = 2 * M * own_modes
    slots = LISTS * CAP
    lists = slabs * LISTS
    points = point_feat.shape[0]

    live = pair_cell[0, :, 0] >= 0
    cells, hot = compact(pair_cell[0], live)
    point_ids, _ = compact(pair_point[0], live)
    own_slab = jnp.sum(jnp.where(hot, jnp.arange(slabs)[None, :], 0), axis=1).astype(jnp.int32)
    cells, point_ids = pad8(cells), pad8(point_ids)
    slab_rows = jnp.broadcast_to(own_slab[:, None], (LISTS, CAP))

    lifted, meta = pl.pallas_call(
        functools.partial(prep_kernel, planes=planes),
        out_shape=(
            jax.ShapeDtypeStruct((C, slots), BF16),
            jax.ShapeDtypeStruct((16, slots), BF16),
        ),
        in_specs=[VMEM] * 6,
        out_specs=(VMEM, VMEM),
        compiler_params=params(),
        name="prep",
    )(point_feat.T, point_pos, point_ids, cells, pad8(slab_rows), lift_weight)

    all_meta = gather(meta, slabs, 0, "gather_meta")

    def keys(values):
        values = values.astype(F32)
        return (values[..., 0, :] * G + values[..., 1, :]) * G + values[..., 2, :]

    key = keys(all_meta).reshape(lists, 1, CAP)
    weight = all_meta[:, 3].astype(F32).reshape(lists, 1, CAP)
    slab_ids = (all_meta[:, 0, ::CAP].astype(jnp.int32) // planes).reshape(lists)
    own_key = pad8(keys(meta).reshape(LISTS, CAP))

    terms, bucket, count = pl.pallas_call(
        share_kernel,
        out_shape=(
            jax.ShapeDtypeStruct((C, slots), BF16),
            jax.ShapeDtypeStruct(((LISTS + 1) * lists,), jnp.int32),
            jax.ShapeDtypeStruct((LISTS,), jnp.int32),
        ),
        in_specs=[SMEM, SMEM, VMEM, VMEM, VMEM, VMEM, VMEM],
        out_specs=(VMEM, SMEM, SMEM),
        compiler_params=params(),
        name="share",
    )(slab_ids, own_slab, key, weight, own_key, meta, lifted)
    all_terms = gather(terms, slabs, 1, "gather_terms")

    cos_y, sin_y = waves(frequencies(M), G)
    cos_z, sin_z = waves(frequencies(own_modes, me * own_modes), G)
    cos_b, sin_b = jnp.repeat(cos_y, own_modes, 0), jnp.repeat(sin_y, own_modes, 0)
    cos_c, sin_c = jnp.tile(cos_z, (2 * M, 1)), jnp.tile(sin_z, (2 * M, 1))
    tab_y = jnp.concatenate([cos_b, -sin_b, -sin_b, -cos_b], 0).astype(BF16)
    tab_z = jnp.concatenate([cos_c, sin_c], 0).astype(BF16)

    def region_block(height):
        return pl.BlockSpec((1, height, slots), lambda r, ids: (r, 0, 0))

    def whole(shape):
        return pl.BlockSpec(shape, lambda r, ids: (0,) * len(shape))

    tab_x = jnp.concatenate([cos_y, sin_y], 0)
    spread, collect = selections(own_modes)
    mixed, wave = pl.pallas_call(
        functools.partial(forward_kernel, planes=planes),
        out_shape=(
            jax.ShapeDtypeStruct((M, C, rows), F32),
            jax.ShapeDtypeStruct((slabs, rows, slots), BF16),
        ),
        grid_spec=pltpu.PrefetchScalarGridSpec(
            num_scalar_prefetch=1,
            grid=(slabs,),
            in_specs=[
                region_block(C),
                region_block(16),
                whole((2 * rows, G)),
                whole((2 * rows, G)),
                whole((2 * M, G)),
                whole(spread.shape),
                whole(collect.shape),
                pl.BlockSpec(memory_space=pl.ANY),
            ],
            out_specs=(whole((M, C, rows)), region_block(rows)),
            scratch_shapes=[
                pltpu.VMEM((G * C, rows), F32),
                pltpu.VMEM((C * M, rows), F32),
                pltpu.VMEM((M, C, rows), BF16),
                pltpu.VMEM((HELD,) + spectral_weight.shape[1:], BF16),
                pltpu.SemaphoreType.DMA((HELD,)),
            ],
        ),
        compiler_params=params(VMEM_MOST),
        name="forward",
    )(slab_ids, all_terms, all_meta, tab_y, tab_z, tab_x.astype(BF16), spread, collect, spectral_weight)

    partial = pl.pallas_call(
        functools.partial(inverse_kernel, planes=planes),
        out_shape=jax.ShapeDtypeStruct((slabs, C, slots), BF16),
        grid_spec=pltpu.PrefetchScalarGridSpec(
            num_scalar_prefetch=1,
            grid=(slabs,),
            in_specs=[
                region_block(16),
                region_block(rows),
                whole((M * C, rows)),
                whole((G, 2 * M)),
            ],
            out_specs=region_block(C),
            scratch_shapes=[pltpu.VMEM((G * C, rows), F32), pltpu.VMEM((G * C, rows), BF16)],
        ),
        compiler_params=params(),
        name="inverse",
    )(slab_ids, all_meta, wave, mixed.reshape(M * C, rows), (tab_x.T / float(G * G * G)).astype(BF16))
    spectral = scatter(partial, slabs, 2, "scatter")

    cell_lifted = pl.pallas_call(
        cell_kernel,
        out_shape=jax.ShapeDtypeStruct((C, slots), F32),
        in_specs=[SMEM, SMEM, VMEM, VMEM, VMEM],
        out_specs=VMEM,
        compiler_params=params(),
        name="cells",
    )(bucket, count, all_terms, key, own_key)

    out = pl.pallas_call(
        decode_kernel,
        out_shape=jax.ShapeDtypeStruct((C, points), BF16),
        in_specs=[VMEM] * 6,
        out_specs=VMEM,
        compiler_params=params(),
        name="decode",
    )(spectral, cell_lifted, meta, point_ids, skip_weight, proj_weight)
    return out.T


def solution(mesh):
    in_specs = (
        P(("groups", "slab"), None),
        P(None, ("groups", "slab")),
        P(("groups", "slab"), None, None),
        P(("groups", "slab"), None, None),
        P(),
        P(None, None, "slab", None, None, None),
        P(),
        P(),
    )
    out_specs = P(("groups", "slab"), None)
    return jax.shard_map(shards, mesh=mesh, in_specs=in_specs, out_specs=out_specs, check_vma=False)
```

```python
import functools

import jax
import jax.numpy as jnp
import numpy as np
from jax import lax
from jax.experimental import pallas as pl
from jax.experimental.pallas import tpu as pltpu
from jax.sharding import PartitionSpec as P

G = 128
C = 64
M = 32
RADIUS = 2
LISTS = 5
CAP = 256
HELD = 20
STEP = 4
SIDE = 4
VMEM_LIMIT = 32 * 1024 * 1024
VMEM_MOST = 58 * 1024 * 1024
F32 = jnp.float32
BF16 = jnp.bfloat16


def params(limit=VMEM_LIMIT):
    return pltpu.CompilerParams(vmem_limit_bytes=limit)


def frequencies(count, first=0):
    k = first + jnp.arange(count)
    return jnp.where(k < M // 2, k, k - M)


def waves(frequency, length):
    phase = (frequency[:, None] * jnp.arange(length)[None, :]) % length
    angle = (2.0 * jnp.pi / length) * phase.astype(F32)
    return jnp.cos(angle), jnp.sin(angle)


def nt_dot(left, right):
    return lax.dot_general(left, right, (((1,), (1,)), ((), ())), preferred_element_type=F32)


def dot(left, right):
    return jnp.dot(left, right, preferred_element_type=F32)


def prep_kernel(feat_ref, pos_ref, point_ref, cell_ref, slab_ref, lift_ref, lifted_ref, meta_ref, planes):
    points = feat_ref.shape[1]
    pos = pos_ref[...]
    high = pos.astype(BF16)
    rest = pos - high.astype(F32)
    middle = rest.astype(BF16)
    low = (rest - middle.astype(F32)).astype(BF16)
    lift = lift_ref[...]
    feat = feat_ref[...]
    for k in range(LISTS):
        place = pl.ds(k * CAP, CAP)
        point = point_ref[k : k + 1, :]
        cell = cell_ref[k : k + 1, :]
        live = cell >= 0
        cell = jnp.maximum(cell, 0)
        rows = lax.broadcasted_iota(jnp.int32, (points, CAP), 0)
        hot = jnp.where(rows == point, 1.0, 0.0).astype(BF16)
        got = dot(feat, hot).astype(BF16)
        lifted_ref[:, place] = lax.dot_general(
            lift, got, (((0,), (0,)), ((), ())), preferred_element_type=F32
        ).astype(BF16)
        at = dot(high, hot) + dot(middle, hot) + dot(low, hot)
        x = cell // (G * G) + slab_ref[k : k + 1, :] * planes
        y = cell // G % G
        z = cell % G
        xf, yf, zf = x.astype(F32), y.astype(F32), z.astype(F32)
        distance = (
            (at[0:1] - (xf + 0.5)) ** 2 + (at[1:2] - (yf + 0.5)) ** 2 + (at[2:3] - (zf + 0.5)) ** 2
        )
        kernel = 1.0 / (1.0 + distance / float(RADIUS * RADIUS))
        weight = jnp.where(live, kernel, 0.0)
        meta_ref[:, place] = jnp.concatenate(
            [xf, yf, zf, weight, jnp.zeros((12, CAP), F32)], axis=0
        ).astype(BF16)


def places(slabs):
    return (slabs // 4, 2) if slabs <= 16 else (slabs // 2, 1)


def peers(depth, width):
    me = lax.axis_index("slab")
    core, y, z = me % 2, (me // 2) % width, me // (2 * width)

    def at(z, y, core):
        return (z * width + y) * 2 + core

    return at, z, y, core


def greet(others):
    barrier = pltpu.get_barrier_semaphore()
    for other in others:
        pl.semaphore_signal(
            barrier, inc=1, device_id={"slab": other}, device_id_type=pl.DeviceIdType.MESH
        )
    pl.semaphore_wait(barrier, len(others))


def remote(source, target, send_sem, recv_sem, other):
    return pltpu.make_async_remote_copy(
        src_ref=source,
        dst_ref=target,
        send_sem=send_sem,
        recv_sem=recv_sem,
        device_id={"slab": other},
        device_id_type=pl.DeviceIdType.MESH,
    )


def gather_kernel(source_ref, out_ref, send_sem, recv_sem, own_sem, depth, width):
    at, z, y, core = peers(depth, width)
    ahead = [at((z + d) % depth, y, core) for d in range(1, depth)]
    beside = at(z, (y + 1) % width, core)
    twin = at(z, y, 1 - core)
    greet(ahead + ([beside] if width > 1 else []) + [twin])
    me = at(z, y, core)
    own = pltpu.make_async_copy(source_ref, out_ref.at[me], own_sem)
    own.start()
    sent = []

    def send(source, block, other):
        copy = remote(source, out_ref.at[block], send_sem.at[len(sent)], recv_sem.at[block], other)
        copy.start()
        sent.append(copy)

    def arrived(block):
        remote(source_ref, out_ref.at[block], send_sem.at[0], recv_sem.at[block], twin).wait_recv()

    for other in ahead:
        send(source_ref, me, other)
    if width > 1:
        send(source_ref, me, beside)
    send(source_ref, me, twin)
    for d in range(1, depth):
        block = at((z + depth - d) % depth, y, core)
        arrived(block)
        if width > 1:
            send(out_ref.at[block], block, beside)
        send(out_ref.at[block], block, twin)
    if width > 1:
        for d in range(depth):
            block = at((z + depth - d) % depth, 1 - y, core)
            arrived(block)
            send(out_ref.at[block], block, twin)
    for d in range(depth):
        for w in range(width):
            arrived(at((z + depth - d) % depth, (y + w) % width, 1 - core))
    own.wait()
    for copy in sent:
        copy.wait_send()


def gather(block, slabs, collective_id, name):
    depth, width = places(slabs)
    return pl.pallas_call(
        functools.partial(gather_kernel, depth=depth, width=width),
        out_shape=jax.ShapeDtypeStruct((slabs,) + block.shape, block.dtype),
        in_specs=[pl.BlockSpec(memory_space=pl.ANY)],
        out_specs=pl.BlockSpec(memory_space=pl.ANY),
        scratch_shapes=[
            pltpu.SemaphoreType.DMA((slabs,)),
            pltpu.SemaphoreType.DMA((slabs,)),
            pltpu.SemaphoreType.DMA,
        ],
        compiler_params=pltpu.CompilerParams(collective_id=collective_id, has_side_effects=True),
        name=name,
    )(block)


def scatter_kernel(
    slab_ref, meta_ref, wave_ref, field_ref, out_ref, blocks, from_core, from_y, from_z, to_y, to_z,
    core_send, core_recv, y_send, y_recv, z_send, z_recv, depth, width, planes,
):
    at, z, y, core = peers(depth, width)
    ahead = [at((z + d) % depth, y, core) for d in range(1, depth)]
    beside = at(z, (y + 1) % width, core)
    twin = at(z, y, 1 - core)
    greet(ahead + ([beside] if width > 1 else []) + [twin])
    order = list(range(1, depth)) + [0]
    core_copies, y_copies, z_copies = {}, {}, {}

    def evaluate(d):
        def one(j, _):
            block = at((z + d) % depth, (y + j) % width, (core + 1 + j // width) % 2)
            for k in range(LISTS):
                place = pl.ds(k * CAP, CAP)
                slab = slab_ref[block * LISTS + k]
                local = meta_ref[block, :, place].astype(F32)[0:1] - (slab * planes).astype(F32)
                values = dot(field_ref[slab], wave_ref[block, :, place])
                total = values[:C]
                for p in range(1, planes):
                    total = jnp.where(local == float(p), values[p * C : (p + 1) * C], total)
                blocks[block, :, place] = total.astype(BF16)
            return 0

        lax.fori_loop(0, 2 * width, one, 0)
        for w in range(width):
            slot = d * width + w
            target = at((z + d) % depth, (y + w) % width, 1 - core)
            core_copies[slot] = remote(
                blocks.at[target], from_core.at[slot], core_send.at[slot], core_recv.at[slot], twin
            )
            core_copies[slot].start()

    def pair(d, w):
        slot = d * width + w
        core_copies[slot].wait_recv()
        own = blocks[at((z + d) % depth, (y + w) % width, core)].astype(F32)
        return own + from_core[slot].astype(F32)

    def along_y(d):
        if width > 1:
            to_y[d] = pair(d, 1).astype(BF16)
            y_copies[d] = remote(to_y.at[d], from_y.at[d], y_send.at[d], y_recv.at[d], beside)
            y_copies[d].start()

    def along_z(d):
        total = pair(d, 0)
        if width > 1:
            y_copies[d].wait_recv()
            total += from_y[d].astype(F32)
        if d > 0:
            to_z[d] = total.astype(BF16)
            z_copies[d] = remote(
                to_z.at[d], from_z.at[d], z_send.at[d], z_recv.at[d], ahead[d - 1]
            )
            z_copies[d].start()
        else:
            out_ref[...] = total

    for n in range(depth + 2):
        if n < depth:
            evaluate(order[n])
        if 0 <= n - 1 < depth:
            along_y(order[n - 1])
        if 0 <= n - 2 < depth:
            along_z(order[n - 2])
    for d in range(1, depth):
        z_copies[d].wait_recv()
        out_ref[...] += from_z[d].astype(F32)
    for copies in (core_copies, y_copies, z_copies):
        for copy in copies.values():
            copy.wait_send()


def scatter(slab_ids, meta, wave, field, planes, collective_id, name):
    slabs, slots = meta.shape[0], meta.shape[2]
    depth, width = places(slabs)
    shape = (C, slots)
    return pl.pallas_call(
        functools.partial(scatter_kernel, depth=depth, width=width, planes=planes),
        out_shape=jax.ShapeDtypeStruct(shape, F32),
        in_specs=[SMEM, VMEM, VMEM, VMEM],
        out_specs=VMEM,
        scratch_shapes=[
            pltpu.VMEM((slabs,) + shape, BF16),
            pltpu.VMEM((depth * width,) + shape, BF16),
            *[pltpu.VMEM((depth,) + shape, BF16)] * 4,
            *[pltpu.SemaphoreType.DMA((depth * width,))] * 2,
            *[pltpu.SemaphoreType.DMA((depth,))] * 4,
        ],
        compiler_params=pltpu.CompilerParams(
            collective_id=collective_id, has_side_effects=True, vmem_limit_bytes=VMEM_LIMIT
        ),
        name=name,
    )(slab_ids, meta, wave, field)


def share_kernel(slab_ref, own_slab_ref, key_ref, weight_ref, own_key_ref, own_meta_ref, lifted_ref, term_ref, bucket, count):
    lists = key_ref.shape[0]
    own = [own_slab_ref[k] for k in range(LISTS)]

    def fill(i, counts):
        s = slab_ref[i]
        for k in range(LISTS):
            bucket[k * lists + counts[k]] = i
        return tuple(n + (s == o).astype(jnp.int32) for n, o in zip(counts, own))

    counts = lax.fori_loop(0, lists, fill, (jnp.int32(0),) * LISTS)
    for k in range(LISTS):
        count[k] = counts[k]
    own_keys = [own_key_ref[k : k + 1, :] for k in range(LISTS)]

    def add(p, totals):
        added = []
        for k in range(LISTS):
            valid = p < counts[k]
            i = jnp.where(valid, bucket[k * lists + p], 0)
            weight = jnp.where(valid, weight_ref[i], 0.0)
            both = jnp.concatenate([key_ref[i], weight, jnp.zeros((6, CAP), F32)], axis=0)
            turned = both.T
            terms = jnp.where(turned[:, 0:1] == own_keys[k], turned[:, 1:2], 0.0)
            added.append(totals[k] + jnp.sum(terms, axis=0, keepdims=True))
        return tuple(added)

    longest = functools.reduce(jnp.maximum, counts)
    totals = lax.fori_loop(0, longest, add, (jnp.zeros((1, CAP), F32),) * LISTS)
    for k in range(LISTS):
        place = pl.ds(k * CAP, CAP)
        weight = own_meta_ref[:, place].astype(F32)[3:4]
        scaled = lifted_ref[:, place].astype(F32) * (weight / (1.0 + totals[k]))
        term_ref[:, place] = scaled.astype(BF16)


def mix_modes(modes, weight_refs, spread_ref, collect_ref):
    columns, own_modes = weight_refs[0].shape[0], weight_refs[0].shape[1]
    depth, height = own_modes * 2 * C, own_modes * 2 * SIDE
    lefts = []
    for mode in modes:
        sides = [nt_dot(spread_ref[i], mode) for i in range(spread_ref.shape[0])]
        lefts.append(jnp.concatenate(sides, axis=1))
    products = []
    for left, weight_ref in zip(lefts, weight_refs):
        blocks = []
        for g in range(columns // SIDE):
            weights = [weight_ref[SIDE * g + i].reshape(depth, C) for i in range(SIDE)]
            rows = slice(height * g, height * (g + 1))
            blocks.append(dot(left[rows].astype(BF16), jnp.concatenate(weights, axis=1)))
        products.append(jnp.concatenate(blocks, axis=0).astype(BF16))
    outs = []
    for product in products:
        turned = lax.dot_general(
            product, collect_ref[...], (((0,), (0,)), ((), ())), preferred_element_type=F32
        )
        lane = lax.broadcasted_iota(jnp.int32, (C, turned.shape[1]), 1)
        side = lane // own_modes % SIDE
        total = turned[:C]
        for i in range(1, SIDE):
            total = jnp.where(side == i, turned[i * C : (i + 1) * C], total)
        outs.append(total)
    return outs


def forward_kernel(
    slab_ref, lifted_ref, meta_ref, tab_y_ref, tab_z_ref, tab_x_ref, spread_ref, collect_ref,
    tab_back_ref, weight_ref, field_ref, wave_ref, total, lines, modes, weights, weight_sem, planes,
):
    region = pl.program_id(0)
    rows = wave_ref.shape[1]
    held = weights.shape[0]

    def fetch(a, slot):
        return pltpu.make_async_copy(weight_ref.at[a], weights.at[slot], weight_sem.at[slot])

    @pl.when(region == 0)
    def _():
        for a in range(held):
            fetch(a, a).start()
        total[...] = jnp.zeros_like(total)

    for k in range(LISTS):
        place = pl.ds(k * CAP, CAP)
        slab = slab_ref[region * LISTS + k]
        meta = meta_ref[0, :, place].astype(F32)
        line = lax.broadcasted_iota(jnp.int32, (G, CAP), 0).astype(F32)
        hot_y = jnp.where(line == meta[1:2], 1.0, 0.0).astype(BF16)
        hot_z = jnp.where(line == meta[2:3], 1.0, 0.0).astype(BF16)
        along_y = dot(tab_y_ref[...], hot_y)
        along_z = dot(tab_z_ref[...], hot_z)
        wave = along_y[:rows] * along_z[:rows] + along_y[rows:] * along_z[rows:]
        wave = wave.astype(BF16)
        wave_ref[0, :, place] = wave
        scaled = lifted_ref[0, :, place]
        local = meta[0:1] - (slab * planes).astype(F32)
        parts = [
            scaled * jnp.where(local == float(p), 1.0, 0.0).astype(BF16) for p in range(planes)
        ]
        height = planes * C
        at = pl.ds(pl.multiple_of(slab * height, height), height)
        total[at, :] += nt_dot(jnp.concatenate(parts, axis=0), wave)

    @pl.when(region == pl.num_programs(0) - 1)
    def _():
        half = rows // 2
        sign = jnp.where(lax.broadcasted_iota(jnp.int32, (M, rows), 1) < half, 1.0, -1.0)

        def along_x(d, _):
            line = total[pl.ds(d, G, stride=C), :].astype(BF16)
            both = dot(tab_x_ref[...], line)
            turned = jnp.concatenate([both[M:, half:], both[M:, :half]], axis=1)
            lines[pl.ds(pl.multiple_of(d * M, M), M), :] = both[:M] + sign * turned
            return 0

        lax.fori_loop(0, C, along_x, 0, unroll=16)
        for a in range(M):
            modes[a] = lines[pl.ds(a, C, stride=M), :].astype(BF16)

        def mix(step, _):
            first = step * STEP
            places = [(first + i) % held for i in range(STEP)]
            for i in range(STEP):
                fetch(first + i, places[i]).wait()
            outs = mix_modes(
                [modes[first + i] for i in range(STEP)],
                [weights.at[place] for place in places],
                spread_ref,
                collect_ref,
            )
            for i in range(STEP):
                at = pl.ds(pl.multiple_of((first + i) * C, C), C)
                lines[at, :] = outs[i]

            @pl.when(first + held < M)
            def _():
                for i in range(STEP):
                    fetch(first + held + i, places[i]).start()

            return 0

        lax.fori_loop(0, M // STEP, mix, 0)

        def back_along_x(e, _):
            line = lines[pl.ds(e, M, stride=C), :]
            turned = -sign * jnp.concatenate([line[:, half:], line[:, :half]], axis=1)
            both = jnp.concatenate([line, turned], axis=0).astype(BF16)
            total[pl.ds(e, G, stride=C), :] = dot(tab_back_ref[...], both)
            return 0

        lax.fori_loop(0, C, back_along_x, 0, unroll=16)
        field_ref[...] = total[...].astype(BF16).reshape(field_ref.shape)


def cell_kernel(bucket, count, lifted_ref, key_ref, own_key_ref, out_ref):
    lists = key_ref.shape[0]
    counts = [count[k] for k in range(LISTS)]
    out_ref[...] = jnp.zeros_like(out_ref)
    turned = [
        jnp.broadcast_to(own_key_ref[k : k + 1, :], (8, CAP)).T[:, 0:1] for k in range(LISTS)
    ]

    def add(p, _):
        for k in range(LISTS):
            valid = p < counts[k]
            i = jnp.where(valid, bucket[k * lists + p], 0)
            key = jnp.where(valid, key_ref[i], -1.0)
            same = jnp.where(turned[k] == key, 1.0, 0.0).astype(BF16)
            slots = pl.ds(pl.multiple_of((i % LISTS) * CAP, CAP), CAP)
            out_ref[:, pl.ds(k * CAP, CAP)] += nt_dot(lifted_ref[i // LISTS, :, slots], same)
        return 0

    lax.fori_loop(0, functools.reduce(jnp.maximum, counts), add, 0)


def decode_kernel(spectral_ref, cell_ref, meta_ref, point_ref, skip_ref, proj_ref, out_ref):
    points = out_ref.shape[1]
    total = jnp.zeros((C + 16, points), F32)
    for k in range(LISTS):
        place = pl.ds(k * CAP, CAP)
        skip = lax.dot_general(
            skip_ref[...],
            cell_ref[:, place].astype(BF16),
            (((0,), (0,)), ((), ())),
            preferred_element_type=F32,
        )
        u = spectral_ref[:, place].astype(F32) + skip
        hidden = 0.5 * u * (1.0 + jnp.tanh(0.7978845608028654 * (u + 0.044715 * u * u * u)))
        hidden = jnp.concatenate([hidden, jnp.ones((16, CAP), F32)], axis=0).astype(BF16)
        weight = meta_ref[:, place].astype(F32)[3:4]
        rows = lax.broadcasted_iota(jnp.int32, (points, CAP), 0)
        hot = jnp.where(rows == point_ref[k : k + 1, :], weight, 0.0).astype(BF16)
        total += nt_dot(hidden, hot)
    mean = (total[:C] / (1.0 + total[C : C + 1])).astype(BF16)
    out_ref[...] = lax.dot_general(
        proj_ref[...], mean, (((0,), (0,)), ((), ())), preferred_element_type=F32
    ).astype(BF16)


def selections(own_modes):
    spread = np.zeros((own_modes, 2, M, 2 * own_modes, 2, M, own_modes), np.float32)
    collect = np.zeros((M, 2 * own_modes, 2, M, own_modes), np.float32)
    for b in range(M):
        for c in range(own_modes):
            for w in range(2):
                collect[b, 2 * c + w, w, b, c] = 1.0
                for s in range(2):
                    spread[c, s, b, 2 * c + w, s ^ w, b, c] = -1.0 if s > w else 1.0
    rows = 2 * M * own_modes
    return (
        jnp.asarray(spread.reshape(2 * own_modes, rows, rows), BF16),
        jnp.asarray(collect.reshape(rows, rows), BF16),
    )


def compact(lists, live):
    rank = jnp.cumsum(live.astype(jnp.int32)) - 1
    hot = live[None, :] & (rank[None, :] == jnp.arange(LISTS)[:, None])
    return jnp.sum(jnp.where(hot[:, :, None], lists[None] + 1, 0), axis=1) - 1, hot


def pad8(array):
    return jnp.concatenate([array, jnp.full((8 - LISTS, array.shape[1]), -1, array.dtype)], axis=0)


VMEM = pl.BlockSpec(memory_space=pltpu.VMEM)
SMEM = pl.BlockSpec(memory_space=pltpu.SMEM)


def shards(
    point_feat,
    point_pos,
    pair_point,
    pair_cell,
    lift_weight,
    spectral_weight,
    skip_weight,
    proj_weight,
):
    slabs = lax.axis_size("slab")
    me = lax.axis_index("slab")
    planes = G // slabs
    own_modes = spectral_weight.shape[2]
    rows = 2 * M * own_modes
    slots = LISTS * CAP
    lists = slabs * LISTS
    points = point_feat.shape[0]

    live = pair_cell[0, :, 0] >= 0
    cells, hot = compact(pair_cell[0], live)
    point_ids, _ = compact(pair_point[0], live)
    own_slab = jnp.sum(jnp.where(hot, jnp.arange(slabs)[None, :], 0), axis=1).astype(jnp.int32)
    cells, point_ids = pad8(cells), pad8(point_ids)
    slab_rows = jnp.broadcast_to(own_slab[:, None], (LISTS, CAP))

    lifted, meta = pl.pallas_call(
        functools.partial(prep_kernel, planes=planes),
        out_shape=(
            jax.ShapeDtypeStruct((C, slots), BF16),
            jax.ShapeDtypeStruct((16, slots), BF16),
        ),
        in_specs=[VMEM] * 6,
        out_specs=(VMEM, VMEM),
        compiler_params=params(),
        name="prep",
    )(point_feat.T, point_pos, point_ids, cells, pad8(slab_rows), lift_weight)

    all_meta = gather(meta, slabs, 0, "gather_meta")

    def keys(values):
        values = values.astype(F32)
        return (values[..., 0, :] * G + values[..., 1, :]) * G + values[..., 2, :]

    key = keys(all_meta).reshape(lists, 1, CAP)
    weight = all_meta[:, 3].astype(F32).reshape(lists, 1, CAP)
    slab_ids = (all_meta[:, 0, ::CAP].astype(jnp.int32) // planes).reshape(lists)
    own_key = pad8(keys(meta).reshape(LISTS, CAP))

    terms, bucket, count = pl.pallas_call(
        share_kernel,
        out_shape=(
            jax.ShapeDtypeStruct((C, slots), BF16),
            jax.ShapeDtypeStruct(((LISTS + 1) * lists,), jnp.int32),
            jax.ShapeDtypeStruct((LISTS,), jnp.int32),
        ),
        in_specs=[SMEM, SMEM, VMEM, VMEM, VMEM, VMEM, VMEM],
        out_specs=(VMEM, SMEM, SMEM),
        compiler_params=params(),
        name="share",
    )(slab_ids, own_slab, key, weight, own_key, meta, lifted)
    all_terms = gather(terms, slabs, 1, "gather_terms")

    cos_y, sin_y = waves(frequencies(M), G)
    cos_z, sin_z = waves(frequencies(own_modes, me * own_modes), G)
    cos_b, sin_b = jnp.repeat(cos_y, own_modes, 0), jnp.repeat(sin_y, own_modes, 0)
    cos_c, sin_c = jnp.tile(cos_z, (2 * M, 1)), jnp.tile(sin_z, (2 * M, 1))
    tab_y = jnp.concatenate([cos_b, -sin_b, -sin_b, -cos_b], 0).astype(BF16)
    tab_z = jnp.concatenate([cos_c, sin_c], 0).astype(BF16)

    def region_block(height):
        return pl.BlockSpec((1, height, slots), lambda r, ids: (r, 0, 0))

    def whole(shape):
        return pl.BlockSpec(shape, lambda r, ids: (0,) * len(shape))

    tab_x = jnp.concatenate([cos_y, sin_y], 0)
    tab_back = (tab_x.T / float(G * G * G)).astype(BF16)
    spread, collect = selections(own_modes)
    field, wave = pl.pallas_call(
        functools.partial(forward_kernel, planes=planes),
        out_shape=(
            jax.ShapeDtypeStruct((slabs, planes * C, rows), BF16),
            jax.ShapeDtypeStruct((slabs, rows, slots), BF16),
        ),
        grid_spec=pltpu.PrefetchScalarGridSpec(
            num_scalar_prefetch=1,
            grid=(slabs,),
            in_specs=[
                region_block(C),
                region_block(16),
                whole((2 * rows, G)),
                whole((2 * rows, G)),
                whole((2 * M, G)),
                whole(spread.shape),
                whole(collect.shape),
                whole((G, 2 * M)),
                pl.BlockSpec(memory_space=pl.ANY),
            ],
            out_specs=(whole((slabs, planes * C, rows)), region_block(rows)),
            scratch_shapes=[
                pltpu.VMEM((G * C, rows), F32),
                pltpu.VMEM((C * M, rows), F32),
                pltpu.VMEM((M, C, rows), BF16),
                pltpu.VMEM((HELD,) + spectral_weight.shape[1:], BF16),
                pltpu.SemaphoreType.DMA((HELD,)),
            ],
        ),
        compiler_params=params(VMEM_MOST),
        name="forward",
    )(slab_ids, all_terms, all_meta, tab_y, tab_z, tab_x.astype(BF16), spread, collect, tab_back, spectral_weight)

    spectral = scatter(slab_ids, all_meta, wave, field, planes, 2, "scatter")

    cell_lifted = pl.pallas_call(
        cell_kernel,
        out_shape=jax.ShapeDtypeStruct((C, slots), F32),
        in_specs=[SMEM, SMEM, VMEM, VMEM, VMEM],
        out_specs=VMEM,
        compiler_params=params(),
        name="cells",
    )(bucket, count, all_terms, key, own_key)

    out = pl.pallas_call(
        decode_kernel,
        out_shape=jax.ShapeDtypeStruct((C, points), BF16),
        in_specs=[VMEM] * 6,
        out_specs=VMEM,
        compiler_params=params(),
        name="decode",
    )(spectral, cell_lifted, meta, point_ids, skip_weight, proj_weight)
    return out.T


def solution(mesh):
    in_specs = (
        P(("groups", "slab"), None),
        P(None, ("groups", "slab")),
        P(("groups", "slab"), None, None),
        P(("groups", "slab"), None, None),
        P(),
        P(None, None, "slab", None, None, None),
        P(),
        P(),
    )
    out_specs = P(("groups", "slab"), None)
    return jax.shard_map(shards, mesh=mesh, in_specs=in_specs, out_specs=out_specs, check_vma=False)
```
